512 devices in a mesh: group: 8 (over y_lo, x), tp: 64 (over z, y_hi, core).
Axes of the slice: x: 4, y: 8 (y_hi: 4, y_lo: 2; y = y_hi * 2 + y_lo), z: 8, core: 2. Of those that a mesh axis runs over, the one named last changes fastest.
Arguments:
- hidden: bfloat16 [1024, 12288], P('group', 'tp')
- q_weight: bfloat16 [12288, 12288], P('group', 'tp'), may hold values from -0.0546875 to 0.0546875
- kv_weight: bfloat16 [12288, 2048], P('group', 'tp'), may hold values from -0.0546875 to 0.0546875
- o_weight: bfloat16 [12288, 12288], P('group', 'tp'), may hold values from -0.3125 to 0.3125
- k_pool: bfloat16 [12288, 32, 1024], P(('group', 'tp'))
- v_pool: bfloat16 [12288, 32, 1024], P(('group', 'tp')), may hold values from -6 to 6
- page_table: int32 [1024, 12], P(('group', 'tp')), may hold values from 0 to 23, as said below
- lengths: int32 [1024], P(('group', 'tp')), may hold values from 1 to 384, as said below
Outputs:
- attended: bfloat16 [1024, 12288], P('group', 'tp')
- new_kv: bfloat16 [1024, 2048], P(('group', 'tp'))
The draws below stay inside these ranges and needn't reach their ends.
Inputs may be any that keep to these rules, and one draw needn't show every extreme that they name: `page_table`: the 2 requests of each aligned block name each of that device's 24 page slots exactly once. `lengths`: the first request of each aligned block of 2 requests has exactly 384 cached tokens.
All inputs are finite; a program needn't handle non-finite values.
Results may differ from the reference program's by a relative error of at most 0.01.
Values may be sent and summed in bfloat16 or wider, within the bound.
No kernel may reach another device: no remote copies, remote signals or barrier semaphores. Data moves between devices by JAX's collectives and lax.ppermute only.
A program may use at most 64 MiB of HBM per device.

```python
import jax
import jax.numpy as jnp
from jax import lax

D = 12288
HEADS = 96
KV = 8
HD = 128
ROWS_DEV = 2
PAGE = 32
PAGES = 12
ALL_ROWS = 1024
POOL = 24
SLOTS = 12288


def draw_hidden(key, part):
    key = jax.random.fold_in(key, 17)
    key_base, key_rows, key_cols = jax.random.split(key, 3)
    base = jax.random.normal(key_base, (ALL_ROWS, D), jnp.float32)
    row_scale = jnp.exp(jax.random.uniform(key_rows, (ALL_ROWS, 1), jnp.float32, 0.0, jnp.log(10.0)))
    col_scale = jnp.exp(jax.random.uniform(key_cols, (1, D), jnp.float32, jnp.log(0.3), jnp.log(3.0)))
    return (base * row_scale * col_scale).astype(jnp.bfloat16)


def draw_k_pool(key, part):
    key = jax.random.fold_in(key, 13)
    key_base = jax.random.fold_in(key, 0)
    base = jax.random.normal(key_base, (SLOTS, PAGE, KV * HD), jnp.float32)
    return base.astype(jnp.bfloat16)


def draw_page_table(key, part):
    key = jax.random.fold_in(key, 11)
    devices = ALL_ROWS // ROWS_DEV
    keys = jax.random.split(key, devices)
    orders = jax.vmap(lambda one: jax.random.permutation(one, POOL))(keys)
    return orders.reshape(ALL_ROWS, PAGES).astype(jnp.int32)


def draw_lengths(key, part):
    key = jax.random.fold_in(key, 7)
    drawn = jax.random.randint(key, (ALL_ROWS,), 1, PAGE * PAGES + 1, jnp.int32)
    first = jnp.arange(ALL_ROWS, dtype=jnp.int32) % ROWS_DEV == 0
    return jnp.where(first, jnp.int32(PAGE * PAGES), drawn).astype(jnp.int32)


def level_of(own_key, extent, shards, smallest, top_value):
    gain, own = 1.0, jax.random.fold_in(own_key, 6)
    for position, parts in shards:
        steps = jnp.exp(jax.random.uniform(jax.random.fold_in(own, position), (parts,), jnp.float32, smallest / len(shards), top_value / len(shards)))
        gain = gain * jnp.repeat(steps, extent[position] // parts).reshape([-1 if axis == position else 1 for axis in range(len(extent))])
    return gain


def bell_draw(key, shape, deviation, reach, pieces=(), kind=jnp.bfloat16):
    gain = level_of(key, shape, pieces, -0.22, 0.18) if pieces else 1.0
    values = jax.random.normal(key, shape, jnp.float32) * deviation * gain
    return jnp.minimum(jnp.maximum(values, -reach), reach).astype(kind)


def setup_inputs(seed: int = 0) -> dict:
    streams_of = jax.random.split(jax.random.key(seed), 9)
    return {
        "hidden": draw_hidden(jax.random.fold_in(streams_of[8], 71), 0),
        "q_weight": bell_draw(streams_of[1], (D, HEADS * HD), D ** -0.5, 0.0546875, ((0, 8), (1, 64))),
        "kv_weight": bell_draw(streams_of[2], (D, 2 * KV * HD), D ** -0.5, 0.0546875, ((0, 8), (1, 64))),
        "o_weight": bell_draw(streams_of[3], (HEADS * HD, D), (HEADS * HD // 32) ** -0.5, 0.3125, ((0, 8), (1, 64))),
        "k_pool": draw_k_pool(jax.random.fold_in(streams_of[8], 71), 0),
        "v_pool": bell_draw(streams_of[5], (SLOTS, PAGE, KV * HD), 1.0, 6.0, ((0, 512),)),
        "page_table": draw_page_table(jax.random.fold_in(streams_of[8], 71), 0),
        "lengths": draw_lengths(jax.random.fold_in(streams_of[8], 71), 0),
    }


eps = 1e-05

def attend_device(item):
    queries, fresh, keys_pool, values_pool, table, lengths = item
    nrows = queries.shape[0]
    kv_width = keys_pool.shape[2]
    kv_heads = kv_width // HD
    per_group = queries.shape[1] // HD // kv_heads
    query = queries.astype(jnp.float32).reshape(nrows, kv_heads, per_group, HD)
    own_keys = fresh[:, :kv_width].astype(jnp.float32).reshape(nrows, kv_heads, HD)
    own_values = fresh[:, kv_width:].astype(jnp.float32).reshape(nrows, kv_heads, HD)
    paged_keys = keys_pool[table].astype(jnp.float32).reshape(nrows, -1, kv_heads, HD)
    paged_values = values_pool[table].astype(jnp.float32).reshape(nrows, -1, kv_heads, HD)
    scale = 1.0 / jnp.sqrt(jnp.float32(HD))
    cached = jnp.einsum('rgph,rcgh->rgpc', query, paged_keys) * scale
    own = jnp.einsum('rgph,rgh->rgp', query, own_keys) * scale
    context = paged_keys.shape[1]
    valid = jnp.arange(context, dtype=jnp.int32)[None, :] < lengths[:, None]
    cached = jnp.where(valid[:, None, None, :], cached, jnp.float32(-1e+30))
    top = jnp.maximum(lax.optimization_barrier(jnp.max(cached, axis=-1)), own)
    exp_cached = jnp.exp(cached - top[..., None])
    exp_own = jnp.exp(own - top)
    total = lax.optimization_barrier(jnp.sum(exp_cached, axis=-1)) + exp_own
    weight_cached = (exp_cached / total[..., None]).astype(jnp.bfloat16).astype(jnp.float32)
    weight_own = (exp_own / total).astype(jnp.bfloat16).astype(jnp.float32)
    mixed = jnp.einsum('rgpc,rcgh->rgph', weight_cached, paged_values)
    mixed = mixed + weight_own[..., None] * own_values[:, :, None, :]
    return mixed.astype(jnp.bfloat16).reshape(nrows, -1)

def reference(hidden, q_weight, kv_weight, o_weight, k_pool, v_pool, page_table, lengths):
    wide = hidden.astype(jnp.float32)
    inv_rms = lax.rsqrt(lax.optimization_barrier(jnp.sum(wide * wide, axis=1, keepdims=True)) / D + eps)
    queries = (jnp.dot(hidden, q_weight, preferred_element_type=jnp.float32) * inv_rms).astype(jnp.bfloat16)
    fresh = (jnp.dot(hidden, kv_weight, preferred_element_type=jnp.float32) * inv_rms).astype(jnp.bfloat16)
    devices = ALL_ROWS // ROWS_DEV
    kv_width = k_pool.shape[2]
    mixed = lax.map(attend_device, (queries.reshape(devices, ROWS_DEV, -1), fresh.reshape(devices, ROWS_DEV, -1), k_pool.reshape(devices, POOL, PAGE, kv_width), v_pool.reshape(devices, POOL, PAGE, kv_width), page_table.reshape(devices, ROWS_DEV, PAGES), lengths.reshape(devices, ROWS_DEV)))
    mixed = mixed.reshape(ALL_ROWS, -1)
    attended = jnp.dot(mixed, o_weight, preferred_element_type=jnp.float32).astype(jnp.bfloat16)
    return (attended, fresh)
```

```python
import jax
import jax.numpy as jnp
from jax import lax
from jax.experimental import pallas as pl
from jax.experimental.pallas import tpu as pltpu
from jax.sharding import Mesh, PartitionSpec as P

D = 12288
HD = 128

eps = 1e-05

G = ("yl", "x")
T = ("zq", "zp", "yh", "c")


def attend_rows(q_rows, kv_rows, k_pool, v_pool, page_table, lengths):
    nrows = q_rows.shape[0]
    kv_width = k_pool.shape[2]
    kv_heads = kv_width // HD
    per_group = q_rows.shape[1] // HD // kv_heads
    query = q_rows.reshape(nrows, kv_heads, per_group, HD)
    own_keys = kv_rows[:, :kv_width].reshape(nrows, kv_heads, HD)
    own_values = kv_rows[:, kv_width:].reshape(nrows, kv_heads, HD)
    paged_keys = k_pool[page_table].reshape(nrows, -1, kv_heads, HD)
    paged_values = v_pool[page_table].reshape(nrows, -1, kv_heads, HD)
    scale = 1.0 / jnp.sqrt(jnp.float32(HD))
    cached = (
        jnp.einsum("rgph,rcgh->rgpc", query, paged_keys, preferred_element_type=jnp.float32) * scale
    )
    own = jnp.einsum("rgph,rgh->rgp", query, own_keys, preferred_element_type=jnp.float32) * scale
    context = paged_keys.shape[1]
    valid = jnp.arange(context, dtype=jnp.int32)[None, :] < lengths[:, None]
    cached = jnp.where(valid[:, None, None, :], cached, jnp.float32(-1e30))
    top = jnp.maximum(jnp.max(cached, axis=-1), own)
    exp_cached = jnp.exp(cached - top[..., None])
    exp_own = jnp.exp(own - top)
    total = jnp.sum(exp_cached, axis=-1) + exp_own
    weight_cached = (exp_cached / total[..., None]).astype(jnp.bfloat16)
    weight_own = (exp_own / total).astype(jnp.bfloat16)
    mixed = jnp.einsum(
        "rgpc,rcgh->rgph", weight_cached, paged_values, preferred_element_type=jnp.float32
    )
    mixed = mixed + weight_own[..., None].astype(jnp.float32) * own_values[:, :, None, :].astype(
        jnp.float32
    )
    return mixed.astype(jnp.bfloat16).reshape(nrows, -1)


def a2a(a, axes):
    return lax.all_to_all(a, axes, split_axis=0, concat_axis=0, tiled=True)


NT = (((1,), (1,)), ((), ()))
VMEM = pl.BlockSpec(memory_space=pltpu.VMEM)
SMEM = pl.BlockSpec(memory_space=pltpu.SMEM)


def limit(mib):
    return pltpu.CompilerParams(vmem_limit_bytes=mib * 2**20)


def split_kernel(place, hidden, *out):
    row = lax.broadcasted_iota(jnp.int32, (128, 128), 0)
    col = lax.broadcasted_iota(jnp.int32, (128, 128), 1)
    zp = (place[2] + row // 64) % 2
    core = (place[1] + row // 32) % 2
    goes = ((row // 8) % 4) * 32 + zp * 16 + ((row // 2) % 4) * 4 + core * 2 + row % 2
    pick = jnp.where(goes == col, 1.0, 0.0).astype(jnp.bfloat16)
    rows = lax.dot_general(pick, hidden[...], NT, preferred_element_type=jnp.float32)
    rows = rows.astype(jnp.bfloat16)
    for k in range(4):
        out[k][...] = rows[k * 32 : k * 32 + 32]


def split(place, hidden):
    return pl.pallas_call(
        split_kernel,
        in_specs=[SMEM, VMEM],
        out_specs=[VMEM] * 4,
        compiler_params=limit(4),
        out_shape=[jax.ShapeDtypeStruct((32, 192), jnp.bfloat16)] * 4,
    )(place, hidden)


def copies_kernel(place, same, core, zp, both, out):
    flip_core, flip_zp = place[1] == 1, place[0] == 1
    blocks = []
    for straight, crossed in ((same, core), (zp, both)):
        first = jnp.where(flip_core, crossed[...], straight[...])
        second = jnp.where(flip_core, straight[...], crossed[...])
        blocks.append(jnp.concatenate([first, second], axis=1))
    first = jnp.where(flip_zp, blocks[1], blocks[0])
    second = jnp.where(flip_zp, blocks[0], blocks[1])
    for to in range(16):
        out[to, :32] = first
        out[to, 32:] = second


def copies(place, parts):
    return pl.pallas_call(
        copies_kernel,
        in_specs=[SMEM] + [VMEM] * 4,
        out_specs=VMEM,
        compiler_params=limit(4),
        out_shape=pltpu.HBM((16, 64, 384), jnp.bfloat16),
    )(place, *parts)


def join_kernel(q, kv, out):
    out[:192] = q[...]
    out[192:] = kv[...]


def join(q, kv):
    return pl.pallas_call(
        join_kernel,
        in_specs=[VMEM] * 2,
        out_specs=VMEM,
        compiler_params=limit(4),
        out_shape=jax.ShapeDtypeStruct((224, 1536), jnp.bfloat16),
    )(q, kv)


def gather_kernel(place, own, near, own_other, near_other, weight):
    zp, core = place[0], place[1]
    for piece, z, c in (
        (own, zp, core),
        (near, 1 - zp, core),
        (own_other, zp, 1 - core),
        (near_other, 1 - zp, 1 - core),
    ):
        at = z * 2 + c
        weight[pl.ds(pl.multiple_of(at * 192, 64), 192), :] = piece[:192]
        weight[pl.ds(pl.multiple_of(768 + at * 32, 32), 32), :] = piece[192:]


def gather(place, pieces):
    return pl.pallas_call(
        gather_kernel,
        in_specs=[SMEM] + [VMEM] * 4,
        out_specs=VMEM,
        out_shape=pltpu.HBM((896, 1536), jnp.bfloat16),
        compiler_params=limit(8),
    )(place, *pieces)


def project_kernel(rows, weight, out):
    total = squares = 0
    for y in range(4):
        a = rows[:, y].reshape(128, 384)
        total += lax.dot_general(
            a, weight[:, y * 384 : y * 384 + 384], NT, preferred_element_type=jnp.float32
        )
        wide = a.astype(jnp.float32)
        squares += jnp.sum(wide * wide, axis=1, keepdims=True)
    out[:, :896] = total.astype(jnp.bfloat16)
    high = squares.astype(jnp.bfloat16).astype(jnp.float32)
    lane = lax.broadcasted_iota(jnp.int32, (128, 128), 1)
    extra = jnp.where(lane == 0, high, jnp.where(lane == 1, squares - high, 0.0))
    out[:, 896:] = extra.astype(jnp.bfloat16)


def project(rows, weight):
    return pl.pallas_call(
        project_kernel,
        grid=(2,),
        in_specs=[
            pl.BlockSpec((2, 4, 64, 384), lambda i: (i, 0, 0, 0)),
            pl.BlockSpec((896, 1536), lambda i: (0, 0)),
        ],
        out_specs=pl.BlockSpec((128, 1024), lambda i: (i, 0)),
        out_shape=pltpu.HBM((256, 1024), jnp.bfloat16),
        compiler_params=limit(12),
        cost_estimate=pl.CostEstimate(
            flops=2 * 256 * 1536 * 896, bytes_accessed=4 * 2**20, transcendentals=0
        ),
    )(rows, weight)


def add_kernel(parts, touch, out):
    del touch
    total = jnp.sum(parts[...].astype(jnp.float32), axis=0)
    squares = jnp.sum(total[:, 896:], axis=1, keepdims=True)
    normed = total[:, :896] * lax.rsqrt(squares / D + eps)
    for r in range(8):
        out[r] = normed[2 * r : 2 * r + 2].astype(jnp.bfloat16)


def add(parts, touch):
    return pl.pallas_call(
        add_kernel,
        grid=(2,),
        in_specs=[
            pl.BlockSpec((8, 16, 1024), lambda i: (0, i, 0)),
            pl.BlockSpec((16, 128), lambda i: (0, 0)),
        ],
        out_specs=pl.BlockSpec((8, 2, 896), lambda i: (i, 0, 0)),
        compiler_params=limit(4),
        out_shape=pltpu.HBM((16, 2, 896), jnp.bfloat16),
    )(parts, touch)


def order_kernel(parts, touch, q, kv):
    del touch
    for z in range(8):
        zq, zp = z // 2, z % 2
        for y in range(4):
            q[z, :, y * 384 : y * 384 + 384] = parts[zq * 4 + y, :, zp * 384 : zp * 384 + 384]
        at = 768 + zp * 64
        for y in range(0, 4, 2):
            pair = [parts[zq * 4 + y + k, :, at : at + 64].astype(jnp.float32) for k in range(2)]
            kv[z, :, y * 64 : y * 64 + 128] = jnp.concatenate(pair, axis=1).astype(jnp.bfloat16)


def order(parts, touch):
    return pl.pallas_call(
        order_kernel,
        in_specs=[VMEM] * 2,
        out_specs=[VMEM] * 2,
        compiler_params=limit(4),
        out_shape=[
            jax.ShapeDtypeStruct((8, 2, 1536), jnp.bfloat16),
            jax.ShapeDtypeStruct((8, 2, 256), jnp.bfloat16),
        ],
    )(parts, touch)


def spread_kernel(place, mine, theirs, own, near_a, near_b, out):
    near = jnp.concatenate([near_a[...], near_b[...]], axis=0)
    for weight, to in ((own[...], place[0]), (near, 1 - place[0])):
        first = lax.dot_general(mine[...], weight, NT, preferred_element_type=jnp.float32)
        second = lax.dot_general(theirs[...], weight, NT, preferred_element_type=jnp.float32)
        first, second = first.astype(jnp.bfloat16), second.astype(jnp.bfloat16)
        last = jnp.concatenate([first[:, 128:], second[:, 128:]], axis=1)
        for g in range(8):
            at = slice(g * 32, g * 32 + 32)
            out[g, to, 0:32, :] = first[at, :128]
            out[g, to, 32:64, :] = second[at, :128]
            out[g, to, 64:96, :] = last[at]


def spread(place, mine, theirs, pieces):
    return pl.pallas_call(
        spread_kernel,
        in_specs=[SMEM] + [VMEM] * 5,
        out_specs=VMEM,
        out_shape=jax.ShapeDtypeStruct((8, 2, 96, 128), jnp.bfloat16),
        compiler_params=limit(16),
        cost_estimate=pl.CostEstimate(
            flops=2 * 512 * 1536 * 384, bytes_accessed=4 * 2**20, transcendentals=0
        ),
    )(place, mine, theirs, *pieces)


def collect_kernel(place, parts, out):
    total = jnp.sum(parts[...].astype(jnp.float32), axis=0).astype(jnp.bfloat16)
    rows = []
    for z in range(2):
        rows.append(jnp.concatenate([total[z, 0:32], total[z, 64:96, :64]], axis=1))
        rows.append(jnp.concatenate([total[z, 32:64], total[z, 64:96, 64:]], axis=1))
    rows = jnp.concatenate(rows, axis=0)
    at = lax.broadcasted_iota(jnp.int32, (128, 128), 0)
    to = lax.broadcasted_iota(jnp.int32, (128, 128), 1)
    core = (place[1] + at // 32) % 2
    goes = ((at // 8) % 4) * 32 + (at // 64) * 16 + ((at // 2) % 4) * 4 + core * 2 + at % 2
    pick = jnp.where(goes == to, 1.0, 0.0).astype(jnp.bfloat16)
    out[...] = lax.dot_general(
        rows, pick, (((0,), (0,)), ((), ())), preferred_element_type=jnp.float32
    ).astype(jnp.bfloat16)


def collect(place, parts):
    return pl.pallas_call(
        collect_kernel,
        in_specs=[SMEM, VMEM],
        out_specs=VMEM,
        compiler_params=limit(4),
        out_shape=jax.ShapeDtypeStruct((192, 128), jnp.bfloat16),
    )(place, parts)


OTHER = [(0, 1), (1, 0)]


def per_device(hidden, q_weight, kv_weight, o_weight, k_pool, v_pool, page_table, lengths):
    place = jnp.stack([lax.axis_index("zp"), lax.axis_index("c"), lax.axis_index("x") % 2])
    place = place.astype(jnp.int32)

    parts = split(place, hidden.T)
    parts = [
        lax.ppermute(
            part,
            G + ("zq", "zp", "c"),
            [
                ((g * 8 + z) * 2 + c, (z * 8 + (g ^ (k // 2))) * 2 + (c ^ (k % 2)))
                for g in range(8)
                for z in range(8)
                for c in range(2)
            ],
        )
        for k, part in enumerate(parts)
    ]

    own = join(q_weight.T, kv_weight.T)
    near = lax.ppermute(own, "zp", OTHER)
    pieces = (own, near, lax.ppermute(own, "c", OTHER), lax.ppermute(near, "c", OTHER))

    rows = a2a(copies(place, parts), ("zq", "yh")).reshape(4, 4, 64, 384)
    o_own = o_weight.T
    o_near = [lax.ppermute(half, "zp", OTHER) for half in (o_own[:96], o_own[96:])]

    parts = a2a(project(rows, gather(place, pieces)).reshape(8, 32, 1024), G)
    parts = a2a(add(parts, o_near[0][:16, :128]), ("zq", "yh"))
    q_rows, kv_rows = order(parts, o_near[1][:16, :128])
    q_rows = q_rows.transpose(1, 0, 2).reshape(2, 12288)
    kv_rows = kv_rows.transpose(1, 0, 2).reshape(2, 2048)

    mixed = attend_rows(q_rows, kv_rows, k_pool, v_pool, page_table, lengths)

    chunks = mixed.reshape(2, 8, 1536).transpose(1, 0, 2)
    send = jnp.broadcast_to(chunks[:, None], (8, 16, 2, 1536)).reshape(128, 2, 1536)
    mine = a2a(send, G + ("zq", "yh")).reshape(256, 1536)
    theirs = lax.ppermute(mine, "c", OTHER)
    out = spread(place, mine, theirs, (o_own, *o_near))
    back = a2a(out.reshape(16, 96, 128), G + ("zp",)).reshape(8, 2, 96, 128)
    return (collect(place, back).T, kv_rows)


def solution(mesh):
    parts = Mesh(mesh.devices.reshape(2, 4, 4, 2, 4, 2), G + T)
    in_specs = (
        P(G, T),
        P(G, T),
        P(G, T),
        P(G, T),
        P(G + T, None, None),
        P(G + T, None, None),
        P(G + T, None),
        P(G + T),
    )
    out_specs = (P(G, T), P(G + T, None))
    return jax.shard_map(
        per_device, mesh=parts, in_specs=in_specs, out_specs=out_specs, check_vma=False
    )
```

```python
import jax
import jax.numpy as jnp
from jax import lax
from jax.experimental import pallas as pl
from jax.experimental.pallas import tpu as pltpu
from jax.sharding import Mesh, PartitionSpec as P

D = 12288
HD = 128

eps = 1e-05

G = ("yl", "x")
T = ("zq", "zp", "yh", "c")


def a2a(a, axes):
    return lax.all_to_all(a, axes, split_axis=0, concat_axis=0, tiled=True)


NT = (((1,), (1,)), ((), ()))
VMEM = pl.BlockSpec(memory_space=pltpu.VMEM)
SMEM = pl.BlockSpec(memory_space=pltpu.SMEM)


def limit(mib):
    return pltpu.CompilerParams(vmem_limit_bytes=mib * 2**20)


def split_kernel(place, hidden, own, other):
    row = lax.broadcasted_iota(jnp.int32, (64, 128), 0)
    col = lax.broadcasted_iota(jnp.int32, (64, 128), 1)
    for out, core in ((own, place[1]), (other, 1 - place[1])):
        goes = ((row // 8) % 4) * 32 + (row // 32) * 16 + ((row // 2) % 4) * 4 + core * 2 + row % 2
        pick = jnp.where(goes == col, 1.0, 0.0).astype(jnp.bfloat16)
        out[...] = lax.dot_general(
            pick, hidden[...], NT, preferred_element_type=jnp.float32
        ).astype(jnp.bfloat16)


def split(place, hidden):
    return pl.pallas_call(
        split_kernel,
        in_specs=[SMEM, VMEM],
        out_specs=[VMEM, VMEM],
        compiler_params=limit(4),
        out_shape=[jax.ShapeDtypeStruct((64, 192), jnp.bfloat16)] * 2,
    )(place, hidden)


def copies_kernel(place, own, other, touch, out):
    del touch
    flip = place[1] == 1
    first = jnp.where(flip, other[...], own[...])
    second = jnp.where(flip, own[...], other[...])
    both = jnp.concatenate([first, second], axis=1)
    for zq in range(4):
        for zp in range(2):
            for y in range(4):
                out[zq * 8 + zp * 4 + y] = both[zp * 32 : zp * 32 + 32]


def copies(place, own, other, touch):
    return pl.pallas_call(
        copies_kernel,
        in_specs=[SMEM] + [VMEM] * 3,
        out_specs=VMEM,
        compiler_params=limit(4),
        out_shape=pltpu.HBM((32, 32, 384), jnp.bfloat16),
    )(place, own, other, touch)


def join_kernel(q, kv, out):
    out[:192] = q[...]
    out[192:] = kv[...]


def join(q, kv):
    return pl.pallas_call(
        join_kernel,
        in_specs=[VMEM] * 2,
        out_specs=VMEM,
        compiler_params=limit(4),
        out_shape=jax.ShapeDtypeStruct((224, 1536), jnp.bfloat16),
    )(q, kv)


def gather_kernel(place, own, near, own_other, near_other, weight):
    zp, core = place[0], place[1]
    for piece, z, c in (
        (own, zp, core),
        (near, 1 - zp, core),
        (own_other, zp, 1 - core),
        (near_other, 1 - zp, 1 - core),
    ):
        at = z * 2 + c
        weight[pl.ds(pl.multiple_of(at * 192, 64), 192), :] = piece[:192]
        weight[pl.ds(pl.multiple_of(768 + at * 32, 32), 32), :] = piece[192:]


def gather(place, pieces):
    return pl.pallas_call(
        gather_kernel,
        in_specs=[SMEM] + [VMEM] * 4,
        out_specs=VMEM,
        out_shape=pltpu.HBM((896, 1536), jnp.bfloat16),
        compiler_params=limit(8),
    )(place, *pieces)


def project_kernel(rows, weight, out):
    total = squares = 0
    for y in range(4):
        a = rows[:, y].reshape(128, 384)
        total += lax.dot_general(
            a, weight[:, y * 384 : y * 384 + 384], NT, preferred_element_type=jnp.float32
        )
        wide = a.astype(jnp.float32)
        squares += jnp.sum(wide * wide, axis=1, keepdims=True)
    out[:, :896] = total.astype(jnp.bfloat16)
    high = squares.astype(jnp.bfloat16).astype(jnp.float32)
    lane = lax.broadcasted_iota(jnp.int32, (128, 128), 1)
    extra = jnp.where(lane == 0, high, jnp.where(lane == 1, squares - high, 0.0))
    out[:, 896:] = extra.astype(jnp.bfloat16)


def project(rows, weight):
    return pl.pallas_call(
        project_kernel,
        grid=(2,),
        in_specs=[
            pl.BlockSpec((4, 4, 32, 384), lambda i: (i, 0, 0, 0)),
            pl.BlockSpec((896, 1536), lambda i: (0, 0)),
        ],
        out_specs=pl.BlockSpec((128, 1024), lambda i: (i, 0)),
        out_shape=pltpu.HBM((256, 1024), jnp.bfloat16),
        compiler_params=limit(12),
        cost_estimate=pl.CostEstimate(
            flops=2 * 256 * 1536 * 896, bytes_accessed=4 * 2**20, transcendentals=0
        ),
    )(rows, weight)


def add_kernel(parts, touch, out):
    del touch
    total = jnp.sum(parts[...].astype(jnp.float32), axis=0)
    squares = jnp.sum(total[:, 896:], axis=1, keepdims=True)
    normed = total[:, :896] * lax.rsqrt(squares / D + eps)
    for r in range(8):
        out[r] = normed[2 * r : 2 * r + 2].astype(jnp.bfloat16)


def add(parts, touch):
    return pl.pallas_call(
        add_kernel,
        grid=(2,),
        in_specs=[
            pl.BlockSpec((8, 16, 1024), lambda i: (0, i, 0)),
            pl.BlockSpec((16, 128), lambda i: (0, 0)),
        ],
        out_specs=pl.BlockSpec((8, 2, 896), lambda i: (i, 0, 0)),
        compiler_params=limit(4),
        out_shape=pltpu.HBM((16, 2, 896), jnp.bfloat16),
    )(parts, touch)


def attend_kernel(table, lengths, parts, k_pool, v_pool, touch, new_kv, send, query, mixed, sem):
    del touch
    row = lax.broadcasted_iota(jnp.int32, (24, 768), 0) % 2
    lane = lax.broadcasted_iota(jnp.int32, (1, 768), 1)
    masks = []
    for r in range(2):
        mask = jnp.zeros((1, 768), jnp.int32)
        for page in range(12):
            start = table[r, page] * 32
            end = start + jnp.clip(lengths[r] - page * 32, 0, 32)
            mask = jnp.where((lane >= start) & (lane < end), 1, mask)
        masks.append(mask)
    valid = jnp.where(row == 0, masks[0], masks[1]) == 1

    for z in range(8):
        zq, zp = z // 2, z % 2
        for y in range(4):
            for k in range(3):
                at, h = zp * 384 + k * 128, y * 3 + k
                query[z, 2 * h : 2 * h + 2, :] = parts[zq * 4 + y, :, at : at + 128].astype(
                    jnp.float32
                )
    fresh = []
    for z in range(8):
        at = 768 + (z % 2) * 64
        for y in range(0, 4, 2):
            pair = [
                parts[(z // 2) * 4 + y + k, :, at : at + 64].astype(jnp.float32) for k in range(2)
            ]
            fresh.append(jnp.concatenate(pair, axis=1))
            to = z * 256 + y * 64
            new_kv[:, to : to + 128] = fresh[-1].astype(jnp.bfloat16)

    scale = 1.0 / jnp.sqrt(jnp.float32(HD))
    odd = lax.broadcasted_iota(jnp.int32, (24, 128), 0) % 2 == 1
    for g in range(8):
        heads = slice(g * 128, g * 128 + 128)
        keys = k_pool[:, :, heads].reshape(768, 128)
        values = v_pool[:, :, heads].reshape(768, 128)
        own_key = jnp.where(odd, fresh[g][1:2], fresh[g][0:1])
        own_value = jnp.where(odd, fresh[8 + g][1:2], fresh[8 + g][0:1])
        q = query[g]
        scores = lax.dot_general(
            q.astype(jnp.bfloat16), keys, NT, preferred_element_type=jnp.float32
        )
        scores = jnp.where(valid, scores * scale, jnp.float32(-1e30))
        own = jnp.sum(q * own_key, axis=1, keepdims=True) * scale
        top = jnp.maximum(jnp.max(scores, axis=1, keepdims=True), own)
        scores = jnp.exp(scores - top)
        own = jnp.exp(own - top)
        total = jnp.sum(scores, axis=1, keepdims=True) + own
        weights = (scores / total).astype(jnp.bfloat16)
        own = (own / total).astype(jnp.bfloat16).astype(jnp.float32)
        out = lax.dot_general(
            weights, values, (((1,), (0,)), ((), ())), preferred_element_type=jnp.float32
        )
        out = out + own * own_value
        for h in range(12):
            mixed[g, :, h * 128 : h * 128 + 128] = out[2 * h : 2 * h + 2].astype(jnp.bfloat16)
    copies = [pltpu.make_async_copy(mixed, send.at[:, k], sem.at[k]) for k in range(16)]
    for copy in copies:
        copy.start()
    for copy in copies:
        copy.wait()


def attend(table, lengths, parts, k_pool, v_pool, touch):
    return pl.pallas_call(
        attend_kernel,
        in_specs=[SMEM] * 2 + [VMEM] * 4,
        out_specs=[VMEM, pl.BlockSpec(memory_space=pl.ANY)],
        out_shape=[
            jax.ShapeDtypeStruct((2, 2048), jnp.bfloat16),
            pltpu.HBM((8, 16, 2, 1536), jnp.bfloat16),
        ],
        scratch_shapes=[
            pltpu.VMEM((8, 24, 128), jnp.float32),
            pltpu.VMEM((8, 2, 1536), jnp.bfloat16),
            pltpu.SemaphoreType.DMA((16,)),
        ],
        compiler_params=limit(16),
    )(table, lengths, parts, k_pool, v_pool, touch)


def spread_kernel(place, mine, theirs, own, near_a, near_b, out):
    near = jnp.concatenate([near_a[...], near_b[...]], axis=0)
    for weight, to in ((own[...], place[0]), (near, 1 - place[0])):
        first = lax.dot_general(mine[...], weight, NT, preferred_element_type=jnp.float32)
        second = lax.dot_general(theirs[...], weight, NT, preferred_element_type=jnp.float32)
        first, second = first.astype(jnp.bfloat16), second.astype(jnp.bfloat16)
        last = jnp.concatenate([first[:, 128:], second[:, 128:]], axis=1)
        for g in range(8):
            at = slice(g * 32, g * 32 + 32)
            out[g, to, 0:32, :] = first[at, :128]
            out[g, to, 32:64, :] = second[at, :128]
            out[g, to, 64:96, :] = last[at]


def spread(place, mine, theirs, pieces):
    return pl.pallas_call(
        spread_kernel,
        in_specs=[SMEM] + [VMEM] * 5,
        out_specs=VMEM,
        out_shape=jax.ShapeDtypeStruct((8, 2, 96, 128), jnp.bfloat16),
        compiler_params=limit(16),
        cost_estimate=pl.CostEstimate(
            flops=2 * 512 * 1536 * 384, bytes_accessed=4 * 2**20, transcendentals=0
        ),
    )(place, mine, theirs, *pieces)


def collect_kernel(place, parts, out):
    total = jnp.sum(parts[...].astype(jnp.float32), axis=0).astype(jnp.bfloat16)
    rows = []
    for z in range(2):
        rows.append(jnp.concatenate([total[z, 0:32], total[z, 64:96, :64]], axis=1))
        rows.append(jnp.concatenate([total[z, 32:64], total[z, 64:96, 64:]], axis=1))
    rows = jnp.concatenate(rows, axis=0)
    at = lax.broadcasted_iota(jnp.int32, (128, 128), 0)
    to = lax.broadcasted_iota(jnp.int32, (128, 128), 1)
    core = (place[1] + at // 32) % 2
    goes = ((at // 8) % 4) * 32 + (at // 64) * 16 + ((at // 2) % 4) * 4 + core * 2 + at % 2
    pick = jnp.where(goes == to, 1.0, 0.0).astype(jnp.bfloat16)
    out[...] = lax.dot_general(
        rows, pick, (((0,), (0,)), ((), ())), preferred_element_type=jnp.float32
    ).astype(jnp.bfloat16)


def collect(place, parts):
    return pl.pallas_call(
        collect_kernel,
        in_specs=[SMEM, VMEM],
        out_specs=VMEM,
        compiler_params=limit(4),
        out_shape=jax.ShapeDtypeStruct((192, 128), jnp.bfloat16),
    )(place, parts)


OTHER = [(0, 1), (1, 0)]


def per_device(hidden, q_weight, kv_weight, o_weight, k_pool, v_pool, page_table, lengths):
    place = jnp.stack([lax.axis_index("zp"), lax.axis_index("c")])
    place = place.astype(jnp.int32)

    own = join(q_weight.T, kv_weight.T)
    near = lax.ppermute(own, "zp", OTHER)
    pieces = (own, near, lax.ppermute(own, "c", OTHER), lax.ppermute(near, "c", OTHER))

    rows = [
        lax.ppermute(
            part,
            G + ("zq", "zp", "c"),
            [
                ((g * 8 + z) * 2 + c, (z * 8 + g) * 2 + (c ^ flip))
                for g in range(8)
                for z in range(8)
                for c in range(2)
            ],
        )
        for flip, part in enumerate(split(place, hidden.T))
    ]
    rows = a2a(copies(place, *rows, near[:16, :128]), ("zq", "zp", "yh")).reshape(8, 4, 32, 384)
    o_own = o_weight.T
    o_near = [lax.ppermute(half, "zp", OTHER) for half in (o_own[:96], o_own[96:])]

    parts = a2a(project(rows, gather(place, pieces)).reshape(8, 32, 1024), G)
    parts = a2a(add(parts, o_near[0][:16, :128]), ("zq", "yh"))
    kv_rows, send = attend(page_table, lengths, parts, k_pool, v_pool, o_near[1][:16, :128])

    mine = a2a(send.reshape(128, 2, 1536), G + ("zq", "yh")).reshape(256, 1536)
    theirs = lax.ppermute(mine, "c", OTHER)
    out = spread(place, mine, theirs, (o_own, *o_near))
    back = a2a(out.reshape(16, 96, 128), G + ("zp",)).reshape(8, 2, 96, 128)
    return (collect(place, back).T, kv_rows)


def solution(mesh):
    parts = Mesh(mesh.devices.reshape(2, 4, 4, 2, 4, 2), G + T)
    in_specs = (
        P(G, T),
        P(G, T),
        P(G, T),
        P(G, T),
        P(G + T, None, None),
        P(G + T, None, None),
        P(G + T, None),
        P(G + T),
    )
    out_specs = (P(G, T), P(G + T, None))
    return jax.shard_map(
        per_device, mesh=parts, in_specs=in_specs, out_specs=out_specs, check_vma=False
    )
```

```python
import jax
import jax.numpy as jnp
from jax import lax
from jax.experimental import pallas as pl
from jax.experimental.pallas import tpu as pltpu
from jax.sharding import Mesh, PartitionSpec as P

D = 12288
HD = 128

eps = 1e-05

G = ("yl", "x")
T = ("zq", "zp", "yh", "c")


def a2a(a, axes):
    return lax.all_to_all(a, axes, split_axis=0, concat_axis=0, tiled=True)


NT = (((1,), (1,)), ((), ()))
VMEM = pl.BlockSpec(memory_space=pltpu.VMEM)
SMEM = pl.BlockSpec(memory_space=pltpu.SMEM)


def in_hbm(a):
    return pltpu.with_memory_space_constraint(a, pltpu.HBM)


def limit(mib):
    return pltpu.CompilerParams(vmem_limit_bytes=mib * 2**20)


def split_kernel(place, hidden, own, other):
    row = lax.broadcasted_iota(jnp.int32, (64, 128), 0)
    col = lax.broadcasted_iota(jnp.int32, (64, 128), 1)
    for out, core in ((own, place[1]), (other, 1 - place[1])):
        goes = ((row // 8) % 4) * 32 + (row // 32) * 16 + ((row // 2) % 4) * 4 + core * 2 + row % 2
        pick = jnp.where(goes == col, 1.0, 0.0).astype(jnp.bfloat16)
        out[...] = lax.dot_general(
            pick, hidden[...], NT, preferred_element_type=jnp.float32
        ).astype(jnp.bfloat16)


def split(place, hidden):
    return pl.pallas_call(
        split_kernel,
        in_specs=[SMEM, VMEM],
        out_specs=[VMEM, VMEM],
        compiler_params=limit(4),
        out_shape=[jax.ShapeDtypeStruct((64, 192), jnp.bfloat16)] * 2,
    )(place, in_hbm(hidden))


def copies_kernel(place, own, other, touch, out):
    del touch
    flip = place[1] == 1
    first = jnp.where(flip, other[...], own[...])
    second = jnp.where(flip, own[...], other[...])
    both = jnp.concatenate([first, second], axis=1)
    for zq in range(4):
        for zp in range(2):
            for y in range(4):
                out[zq * 8 + zp * 4 + y] = both[zp * 32 : zp * 32 + 32]


def copies(place, own, other, touch):
    return pl.pallas_call(
        copies_kernel,
        in_specs=[SMEM] + [VMEM] * 3,
        out_specs=VMEM,
        compiler_params=limit(4),
        out_shape=pltpu.HBM((32, 32, 384), jnp.bfloat16),
    )(place, own, other, touch)


def join_kernel(q, kv, first, second):
    first[...] = q[:112]
    second[:80] = q[112:]
    second[80:] = kv[...]


def join(q, kv):
    return pl.pallas_call(
        join_kernel,
        in_specs=[VMEM] * 2,
        out_specs=[VMEM] * 2,
        compiler_params=limit(4),
        out_shape=[jax.ShapeDtypeStruct((112, 1536), jnp.bfloat16)] * 2,
    )(in_hbm(q), in_hbm(kv))


def gather_kernel(place, *refs):
    zp, core = place[0], place[1]
    weight = refs[8]
    for k, (z, c) in enumerate(((zp, core), (1 - zp, core), (zp, 1 - core), (1 - zp, 1 - core))):
        first, second = refs[2 * k], refs[2 * k + 1]
        at = pl.multiple_of((z * 2 + c) * 192, 64)
        weight[pl.ds(at, 112), :] = first[...]
        weight[pl.ds(pl.multiple_of(at + 112, 16), 80), :] = second[:80]
        at = 768 + (z * 2 + c) * 32
        weight[pl.ds(pl.multiple_of(at, 32), 32), :] = second[80:]


def gather(place, pieces):
    return pl.pallas_call(
        gather_kernel,
        in_specs=[SMEM] + [VMEM] * 8,
        out_specs=VMEM,
        out_shape=pltpu.HBM((896, 1536), jnp.bfloat16),
        compiler_params=limit(8),
    )(place, *pieces)


def project_kernel(rows, weight, out, total, squares):
    step = pl.program_id(0)

    @pl.when(step == 0)
    def _():
        total[...] = jnp.zeros_like(total)
        squares[...] = jnp.zeros_like(squares)

    a = rows[:, 0].reshape(256, 384)
    total[...] += lax.dot_general(a, weight[...], NT, preferred_element_type=jnp.float32)
    wide = a.astype(jnp.float32)
    wide = wide * wide
    squares[...] += wide[:, :128] + wide[:, 128:256] + wide[:, 256:]

    @pl.when(step == 3)
    def _():
        out[:, :896] = total[...].astype(jnp.bfloat16)
        sums = jnp.sum(squares[...], axis=1, keepdims=True)
        high = sums.astype(jnp.bfloat16).astype(jnp.float32)
        lane = lax.broadcasted_iota(jnp.int32, (256, 128), 1)
        extra = jnp.where(lane == 0, high, jnp.where(lane == 1, sums - high, 0.0))
        out[:, 896:] = extra.astype(jnp.bfloat16)


def project(rows, weight):
    return pl.pallas_call(
        project_kernel,
        grid=(4,),
        in_specs=[
            pl.BlockSpec((8, 1, 32, 384), lambda i: (0, i, 0, 0)),
            pl.BlockSpec((896, 384), lambda i: (0, i)),
        ],
        out_specs=pl.BlockSpec((256, 1024), lambda i: (0, 0)),
        out_shape=pltpu.HBM((256, 1024), jnp.bfloat16),
        scratch_shapes=[pltpu.VMEM((256, 896), jnp.float32), pltpu.VMEM((256, 128), jnp.float32)],
        compiler_params=limit(12),
        cost_estimate=pl.CostEstimate(
            flops=2 * 256 * 1536 * 896, bytes_accessed=4 * 2**20, transcendentals=0
        ),
    )(rows, in_hbm(weight))


def add_kernel(parts, out):
    total = jnp.sum(parts[...].astype(jnp.float32), axis=0)
    squares = jnp.sum(total[:, 896:], axis=1, keepdims=True)
    normed = total[:, :896] * lax.rsqrt(squares / D + eps)
    for r in range(8):
        out[r] = normed[2 * r : 2 * r + 2].astype(jnp.bfloat16)


def add(parts):
    return pl.pallas_call(
        add_kernel,
        grid=(2,),
        in_specs=[
            pl.BlockSpec((8, 16, 1024), lambda i: (0, i, 0)),
        ],
        out_specs=pl.BlockSpec((8, 2, 896), lambda i: (i, 0, 0)),
        compiler_params=limit(4),
        out_shape=pltpu.HBM((16, 2, 896), jnp.bfloat16),
    )(parts)


def attend_kernel(table, lengths, parts, k_pool, v_pool, touch, new_kv, send, query, mixed, v_held, sem, v_sem):
    del touch
    fetch = pltpu.make_async_copy(v_pool, v_held, v_sem)
    fetch.start()
    row = lax.broadcasted_iota(jnp.int32, (24, 768), 0) % 2
    lane = lax.broadcasted_iota(jnp.int32, (1, 768), 1)
    masks = []
    for r in range(2):
        mask = jnp.zeros((1, 768), jnp.int32)
        for page in range(12):
            start = table[r, page] * 32
            end = start + jnp.clip(lengths[r] - page * 32, 0, 32)
            mask = jnp.where((lane >= start) & (lane < end), 1, mask)
        masks.append(mask)
    valid = jnp.where(row == 0, masks[0], masks[1]) == 1

    for z in range(8):
        zq, zp = z // 2, z % 2
        for y in range(4):
            for k in range(3):
                at, h = zp * 384 + k * 128, y * 3 + k
                query[z, 2 * h : 2 * h + 2, :] = parts[zq * 4 + y, :, at : at + 128].astype(
                    jnp.float32
                )
    fresh = []
    for z in range(8):
        at = 768 + (z % 2) * 64
        for y in range(0, 4, 2):
            pair = [
                parts[(z // 2) * 4 + y + k, :, at : at + 64].astype(jnp.float32) for k in range(2)
            ]
            fresh.append(jnp.concatenate(pair, axis=1))
            to = z * 256 + y * 64
            new_kv[:, to : to + 128] = fresh[-1].astype(jnp.bfloat16)

    scale = 1.0 / jnp.sqrt(jnp.float32(HD))
    odd = lax.broadcasted_iota(jnp.int32, (24, 128), 0) % 2 == 1
    found = []
    for g in range(8):
        keys = k_pool[:, :, g * 128 : g * 128 + 128].reshape(768, 128)
        own_key = jnp.where(odd, fresh[g][1:2], fresh[g][0:1])
        q = query[g]
        scores = lax.dot_general(
            q.astype(jnp.bfloat16), keys, NT, preferred_element_type=jnp.float32
        )
        scores = jnp.where(valid, scores * scale, jnp.float32(-1e30))
        own = jnp.sum(q * own_key, axis=1, keepdims=True) * scale
        top = jnp.maximum(jnp.max(scores, axis=1, keepdims=True), own)
        scores = jnp.exp(scores - top)
        own = jnp.exp(own - top)
        total = jnp.sum(scores, axis=1, keepdims=True) + own
        weights = (scores / total).astype(jnp.bfloat16)
        found.append((weights, (own / total).astype(jnp.bfloat16).astype(jnp.float32)))
    fetch.wait()
    for g, (weights, own) in enumerate(found):
        values = v_held[:, :, g * 128 : g * 128 + 128].reshape(768, 128)
        own_value = jnp.where(odd, fresh[8 + g][1:2], fresh[8 + g][0:1])
        out = lax.dot_general(
            weights, values, (((1,), (0,)), ((), ())), preferred_element_type=jnp.float32
        )
        out = out + own * own_value
        for h in range(12):
            mixed[g, :, h * 128 : h * 128 + 128] = out[2 * h : 2 * h + 2].astype(jnp.bfloat16)
    copies = [pltpu.make_async_copy(mixed, send.at[:, k], sem.at[k]) for k in range(16)]
    for copy in copies:
        copy.start()
    for copy in copies:
        copy.wait()


def attend(table, lengths, parts, k_pool, v_pool, touch):
    return pl.pallas_call(
        attend_kernel,
        in_specs=[SMEM] * 2 + [VMEM] * 2 + [pl.BlockSpec(memory_space=pl.ANY), VMEM],
        out_specs=[VMEM, pl.BlockSpec(memory_space=pl.ANY)],
        out_shape=[
            jax.ShapeDtypeStruct((2, 2048), jnp.bfloat16),
            pltpu.HBM((8, 16, 2, 1536), jnp.bfloat16),
        ],
        scratch_shapes=[
            pltpu.VMEM((8, 24, 128), jnp.float32),
            pltpu.VMEM((8, 2, 1536), jnp.bfloat16),
            pltpu.VMEM((24, 32, 1024), jnp.bfloat16),
            pltpu.SemaphoreType.DMA((16,)),
            pltpu.SemaphoreType.DMA,
        ],
        compiler_params=limit(16),
    )(table, lengths, parts, k_pool, in_hbm(v_pool), touch)


def spread_kernel(place, rows, *refs):
    zp, core = place[0], place[1]
    out = refs[6]
    pieces = [refs[0][...], jnp.concatenate([refs[1][...], refs[2][...]], axis=0)]
    pieces += [refs[3][...], jnp.concatenate([refs[4][...], refs[5][...]], axis=0)]
    for k, weight in enumerate(pieces):
        z = zp if k % 2 == 0 else 1 - zp
        c = core if k < 2 else 1 - core
        part = lax.dot_general(rows[...], weight, NT, preferred_element_type=jnp.float32)
        part = part.astype(jnp.bfloat16)
        for g in range(8):
            at = g * 32
            out[g, z * 2 + c, 0:32, :] = part[at : at + 32, :128]
            out[g, z * 2 + c, 32:48, :] = jnp.concatenate(
                [part[at : at + 16, 128:], part[at + 16 : at + 32, 128:]], axis=1
            )


def spread(place, rows, pieces):
    return pl.pallas_call(
        spread_kernel,
        in_specs=[SMEM] + [VMEM] * 7,
        out_specs=VMEM,
        out_shape=jax.ShapeDtypeStruct((8, 4, 48, 128), jnp.bfloat16),
        compiler_params=limit(16),
        cost_estimate=pl.CostEstimate(
            flops=2 * 256 * 1536 * 768, bytes_accessed=4 * 2**20, transcendentals=0
        ),
    )(place, rows, *pieces)


def collect_kernel(parts, out):
    total = jnp.sum(parts[...].astype(jnp.float32), axis=0).astype(jnp.bfloat16)
    rows = []
    for k in range(4):
        last = jnp.concatenate([total[k, 32:48, :64], total[k, 32:48, 64:]], axis=0)
        rows.append(jnp.concatenate([total[k, 0:32], last], axis=1))
    rows = jnp.concatenate(rows, axis=0)
    at = lax.broadcasted_iota(jnp.int32, (128, 128), 0)
    to = lax.broadcasted_iota(jnp.int32, (128, 128), 1)
    goes = ((at // 8) % 4) * 32 + (at // 64) * 16 + ((at // 2) % 4) * 4 + ((at // 32) % 2) * 2 + at % 2
    pick = jnp.where(goes == to, 1.0, 0.0).astype(jnp.bfloat16)
    out[...] = lax.dot_general(
        rows, pick, (((0,), (0,)), ((), ())), preferred_element_type=jnp.float32
    ).astype(jnp.bfloat16)


def collect(parts):
    return pl.pallas_call(
        collect_kernel,
        in_specs=[VMEM],
        out_specs=VMEM,
        compiler_params=limit(4),
        out_shape=jax.ShapeDtypeStruct((192, 128), jnp.bfloat16),
    )(parts)


OTHER = [(0, 1), (1, 0)]


def per_device(hidden, q_weight, kv_weight, o_weight, k_pool, v_pool, page_table, lengths):
    place = jnp.stack([lax.axis_index("zp"), lax.axis_index("c")])
    place = place.astype(jnp.int32)

    own = join(q_weight.T, kv_weight.T)
    near = [lax.ppermute(part, "zp", OTHER) for part in own]
    pieces = (*own, *near, *(lax.ppermute(part, "c", OTHER) for part in (*own, *near)))

    rows = [
        lax.ppermute(
            part,
            G + ("zq", "zp", "c"),
            [
                ((g * 8 + z) * 2 + c, (z * 8 + g) * 2 + (c ^ flip))
                for g in range(8)
                for z in range(8)
                for c in range(2)
            ],
        )
        for flip, part in enumerate(split(place, hidden.T))
    ]
    rows = a2a(copies(place, *rows, near[0][:16, :128]), ("zq", "zp", "yh")).reshape(8, 4, 32, 384)
    o_own = o_weight.T
    o_near = [lax.ppermute(half, "zp", OTHER) for half in (o_own[:96], o_own[96:])]
    o_pieces = (o_own, *o_near)

    parts = a2a(project(rows, gather(place, pieces)).reshape(8, 32, 1024), G)
    parts = a2a(add(parts), ("zq", "yh"))
    kv_rows, send = attend(page_table, lengths, parts, k_pool, v_pool, o_near[0][:16, :128])

    mine = a2a(send.reshape(128, 2, 1536), G + ("zq", "yh")).reshape(256, 1536)
    out = spread(place, mine, (*o_pieces, *(lax.ppermute(part, "c", OTHER) for part in o_pieces)))
    back = a2a(out.reshape(32, 48, 128), G + ("zp", "c")).reshape(8, 4, 48, 128)
    return (collect(back).T, kv_rows)


def solution(mesh):
    parts = Mesh(mesh.devices.reshape(2, 4, 4, 2, 4, 2), G + T)
    in_specs = (
        P(G, T),
        P(G, T),
        P(G, T),
        P(G, T),
        P(G + T, None, None),
        P(G + T, None, None),
        P(G + T, None),
        P(G + T),
    )
    out_specs = (P(G, T), P(G + T, None))
    return jax.shard_map(
        per_device, mesh=parts, in_specs=in_specs, out_specs=out_specs, check_vma=False
    )
```

```python
import jax
import jax.numpy as jnp
from jax import lax
from jax.experimental import pallas as pl
from jax.experimental.pallas import tpu as pltpu
from jax.sharding import Mesh, PartitionSpec as P

D = 12288
HD = 128

eps = 1e-05

G = ("yl", "x")
T = ("zq", "zp", "yh", "c")


def a2a(a, axes):
    return lax.all_to_all(a, axes, split_axis=0, concat_axis=0, tiled=True)


NT = (((1,), (1,)), ((), ()))
VMEM = pl.BlockSpec(memory_space=pltpu.VMEM)
SMEM = pl.BlockSpec(memory_space=pltpu.SMEM)


def in_hbm(a):
    return pltpu.with_memory_space_constraint(a, pltpu.HBM)


def limit(mib):
    return pltpu.CompilerParams(vmem_limit_bytes=mib * 2**20)


def split_kernel(place, hidden, own, other):
    row = lax.broadcasted_iota(jnp.int32, (64, 128), 0)
    col = lax.broadcasted_iota(jnp.int32, (64, 128), 1)
    for out, core in ((own, place[1]), (other, 1 - place[1])):
        goes = ((row // 8) % 4) * 32 + (row // 32) * 16 + ((row // 2) % 4) * 4 + core * 2 + row % 2
        pick = jnp.where(goes == col, 1.0, 0.0).astype(jnp.bfloat16)
        out[...] = lax.dot_general(
            pick, hidden[...], NT, preferred_element_type=jnp.float32
        ).astype(jnp.bfloat16)


def split(place, hidden):
    return pl.pallas_call(
        split_kernel,
        in_specs=[SMEM, VMEM],
        out_specs=[VMEM, VMEM],
        compiler_params=limit(4),
        out_shape=[jax.ShapeDtypeStruct((64, 192), jnp.bfloat16)] * 2,
    )(place, hidden)


def copies_kernel(place, own, other, touch, out):
    del touch
    flip = place[1] == 1
    first = jnp.where(flip, other[...], own[...])
    second = jnp.where(flip, own[...], other[...])
    both = jnp.concatenate([first, second], axis=1)
    for zq in range(4):
        for zp in range(2):
            for y in range(4):
                out[zq * 8 + zp * 4 + y] = both[zp * 32 : zp * 32 + 32]


def copies(place, own, other, touch):
    return pl.pallas_call(
        copies_kernel,
        in_specs=[SMEM] + [VMEM] * 3,
        out_specs=VMEM,
        compiler_params=limit(4),
        out_shape=pltpu.HBM((32, 32, 384), jnp.bfloat16),
    )(place, own, other, touch)


def join_kernel(q, kv, out):
    out[:192] = q[...]
    out[192:] = kv[...]


def join(q, kv):
    return pl.pallas_call(
        join_kernel,
        in_specs=[VMEM] * 2,
        out_specs=VMEM,
        compiler_params=limit(4),
        out_shape=pltpu.HBM((224, 1536), jnp.bfloat16),
    )(in_hbm(q), in_hbm(kv))


def project_kernel(place, rows, own, near, own_other, near_other, out, weight, sem):
    zp, core = place[0], place[1]
    fetches = []
    for k, (piece, z, c) in enumerate(
        (
            (own, zp, core),
            (near, 1 - zp, core),
            (own_other, zp, 1 - core),
            (near_other, 1 - zp, 1 - core),
        )
    ):
        at = z * 2 + c
        q_rows = pl.ds(pl.multiple_of(at * 192, 64), 192)
        kv_rows = pl.ds(pl.multiple_of(768 + at * 32, 32), 32)
        fetches.append(pltpu.make_async_copy(piece.at[:192], weight.at[q_rows], sem.at[2 * k]))
        fetches.append(
            pltpu.make_async_copy(piece.at[192:], weight.at[kv_rows], sem.at[2 * k + 1])
        )
    for fetch in fetches:
        fetch.start()
    lane = lax.broadcasted_iota(jnp.int32, (128, 128), 1)
    extras = []
    for half in range(2):
        wide = 0
        for y in range(4):
            a = rows[half * 4 : half * 4 + 4, y].reshape(128, 384).astype(jnp.float32)
            a = a * a
            wide += a[:, :128] + a[:, 128:256] + a[:, 256:]
        sums = jnp.sum(wide, axis=1, keepdims=True)
        high = sums.astype(jnp.bfloat16).astype(jnp.float32)
        extras.append(jnp.where(lane == 0, high, jnp.where(lane == 1, sums - high, 0.0)))
    for fetch in fetches:
        fetch.wait()
    for half in range(2):
        total = 0
        for y in range(4):
            total += lax.dot_general(
                rows[half * 4 : half * 4 + 4, y].reshape(128, 384),
                weight[:, y * 384 : y * 384 + 384],
                NT,
                preferred_element_type=jnp.float32,
            )
        for r in range(64):
            at = slice(2 * r, 2 * r + 2)
            out[half * 64 + r, :, :896] = total[at].astype(jnp.bfloat16)
            out[half * 64 + r, :, 896:] = extras[half][at].astype(jnp.bfloat16)


def project(place, rows, pieces):
    return pl.pallas_call(
        project_kernel,
        in_specs=[SMEM, VMEM] + [pl.BlockSpec(memory_space=pl.ANY)] * 4,
        out_specs=VMEM,
        out_shape=pltpu.HBM((128, 2, 1024), jnp.bfloat16),
        scratch_shapes=[pltpu.VMEM((896, 1536), jnp.bfloat16), pltpu.SemaphoreType.DMA((8,))],
        compiler_params=limit(16),
        cost_estimate=pl.CostEstimate(
            flops=2 * 256 * 1536 * 896, bytes_accessed=4 * 2**20, transcendentals=0
        ),
    )(place, rows, *(in_hbm(piece) for piece in pieces))


def attend_kernel(table, lengths, parts, k_pool, v_pool, touch, new_kv, send, query, mixed, v_held, sem, v_sem):
    del touch
    fetch = pltpu.make_async_copy(v_pool, v_held, v_sem)
    fetch.start()
    row = lax.broadcasted_iota(jnp.int32, (24, 768), 0) % 2
    lane = lax.broadcasted_iota(jnp.int32, (1, 768), 1)
    masks = []
    for r in range(2):
        mask = jnp.zeros((1, 768), jnp.int32)
        for page in range(12):
            start = table[r, page] * 32
            end = start + jnp.clip(lengths[r] - page * 32, 0, 32)
            mask = jnp.where((lane >= start) & (lane < end), 1, mask)
        masks.append(mask)
    valid = jnp.where(row == 0, masks[0], masks[1]) == 1

    normed = []
    for k in range(16):
        total = jnp.sum(parts[:, k].astype(jnp.float32), axis=0)
        if k == 0:
            squares = jnp.sum(total[:, 896:], axis=1, keepdims=True)
            inv_rms = lax.rsqrt(squares / D + eps)
        normed.append((total[:, :896] * inv_rms).astype(jnp.bfloat16).astype(jnp.float32))
    for z in range(8):
        zq, zp = z // 2, z % 2
        for y in range(4):
            for k in range(3):
                at, h = zp * 384 + k * 128, y * 3 + k
                query[z, 2 * h : 2 * h + 2, :] = normed[zq * 4 + y][:, at : at + 128]
    fresh = []
    for z in range(8):
        at = 768 + (z % 2) * 64
        for y in range(0, 4, 2):
            pair = [normed[(z // 2) * 4 + y + k][:, at : at + 64] for k in range(2)]
            fresh.append(jnp.concatenate(pair, axis=1))
            to = z * 256 + y * 64
            new_kv[:, to : to + 128] = fresh[-1].astype(jnp.bfloat16)

    scale = 1.0 / jnp.sqrt(jnp.float32(HD))
    odd = lax.broadcasted_iota(jnp.int32, (24, 128), 0) % 2 == 1
    found = []
    for g in range(8):
        keys = k_pool[:, :, g * 128 : g * 128 + 128].reshape(768, 128)
        own_key = jnp.where(odd, fresh[g][1:2], fresh[g][0:1])
        q = query[g]
        scores = lax.dot_general(
            q.astype(jnp.bfloat16), keys, NT, preferred_element_type=jnp.float32
        )
        scores = jnp.where(valid, scores * scale, jnp.float32(-1e30))
        own = jnp.sum(q * own_key, axis=1, keepdims=True) * scale
        top = jnp.maximum(jnp.max(scores, axis=1, keepdims=True), own)
        scores = jnp.exp(scores - top)
        own = jnp.exp(own - top)
        total = jnp.sum(scores, axis=1, keepdims=True) + own
        weights = (scores / total).astype(jnp.bfloat16)
        found.append((weights, (own / total).astype(jnp.bfloat16).astype(jnp.float32)))
    fetch.wait()
    for g, (weights, own) in enumerate(found):
        values = v_held[:, :, g * 128 : g * 128 + 128].reshape(768, 128)
        own_value = jnp.where(odd, fresh[8 + g][1:2], fresh[8 + g][0:1])
        out = lax.dot_general(
            weights, values, (((1,), (0,)), ((), ())), preferred_element_type=jnp.float32
        )
        out = out + own * own_value
        for h in range(12):
            mixed[g, :, h * 128 : h * 128 + 128] = out[2 * h : 2 * h + 2].astype(jnp.bfloat16)
    copies = [pltpu.make_async_copy(mixed, send.at[:, k], sem.at[k]) for k in range(16)]
    for copy in copies:
        copy.start()
    for copy in copies:
        copy.wait()


def attend(table, lengths, parts, k_pool, v_pool, touch):
    return pl.pallas_call(
        attend_kernel,
        in_specs=[SMEM] * 2 + [VMEM] * 2 + [pl.BlockSpec(memory_space=pl.ANY), VMEM],
        out_specs=[VMEM, pl.BlockSpec(memory_space=pl.ANY)],
        out_shape=[
            jax.ShapeDtypeStruct((2, 2048), jnp.bfloat16),
            pltpu.HBM((8, 16, 2, 1536), jnp.bfloat16),
        ],
        scratch_shapes=[
            pltpu.VMEM((8, 24, 128), jnp.float32),
            pltpu.VMEM((8, 2, 1536), jnp.bfloat16),
            pltpu.VMEM((24, 32, 1024), jnp.bfloat16),
            pltpu.SemaphoreType.DMA((16,)),
            pltpu.SemaphoreType.DMA,
        ],
        compiler_params=limit(16),
    )(table, lengths, parts, k_pool, in_hbm(v_pool), touch)


def spread_kernel(place, mine, theirs, own, near, out):
    for piece, to in ((own, place[0]), (near, 1 - place[0])):
        weight = piece[...]
        first = lax.dot_general(mine[...], weight, NT, preferred_element_type=jnp.float32)
        second = lax.dot_general(theirs[...], weight, NT, preferred_element_type=jnp.float32)
        first, second = first.astype(jnp.bfloat16), second.astype(jnp.bfloat16)
        last = jnp.concatenate([first[:, 128:], second[:, 128:]], axis=1)
        for g in range(8):
            at = slice(g * 32, g * 32 + 32)
            out[g, to, 0:32, :] = first[at, :128]
            out[g, to, 32:64, :] = second[at, :128]
            out[g, to, 64:96, :] = last[at]


def spread(place, mine, theirs, pieces):
    return pl.pallas_call(
        spread_kernel,
        in_specs=[SMEM] + [VMEM] * 4,
        out_specs=VMEM,
        out_shape=jax.ShapeDtypeStruct((8, 2, 96, 128), jnp.bfloat16),
        compiler_params=limit(16),
        cost_estimate=pl.CostEstimate(
            flops=2 * 512 * 1536 * 384, bytes_accessed=4 * 2**20, transcendentals=0
        ),
    )(place, mine, theirs, *pieces)


def collect_kernel(place, parts, out):
    total = jnp.sum(parts[...].astype(jnp.float32), axis=0).astype(jnp.bfloat16)
    rows = []
    for z in range(2):
        rows.append(jnp.concatenate([total[z, 0:32], total[z, 64:96, :64]], axis=1))
        rows.append(jnp.concatenate([total[z, 32:64], total[z, 64:96, 64:]], axis=1))
    rows = jnp.concatenate(rows, axis=0)
    at = lax.broadcasted_iota(jnp.int32, (128, 128), 0)
    to = lax.broadcasted_iota(jnp.int32, (128, 128), 1)
    core = (place[1] + at // 32) % 2
    goes = ((at // 8) % 4) * 32 + (at // 64) * 16 + ((at // 2) % 4) * 4 + core * 2 + at % 2
    pick = jnp.where(goes == to, 1.0, 0.0).astype(jnp.bfloat16)
    out[...] = lax.dot_general(
        rows, pick, (((0,), (0,)), ((), ())), preferred_element_type=jnp.float32
    ).astype(jnp.bfloat16)


def collect(place, parts):
    return pl.pallas_call(
        collect_kernel,
        in_specs=[SMEM, VMEM],
        out_specs=VMEM,
        compiler_params=limit(4),
        out_shape=jax.ShapeDtypeStruct((192, 128), jnp.bfloat16),
    )(place, parts)


OTHER = [(0, 1), (1, 0)]


def per_device(hidden, q_weight, kv_weight, o_weight, k_pool, v_pool, page_table, lengths):
    place = jnp.stack([lax.axis_index("zp"), lax.axis_index("c")])
    place = place.astype(jnp.int32)

    swap = [(g * 8 + z, z * 8 + g) for g in range(8) for z in range(8)]
    own, other = split(place, lax.ppermute(hidden.T, G + ("zq", "zp"), swap))
    other = lax.ppermute(other, "c", OTHER)

    piece = join(q_weight.T, kv_weight.T)
    near = lax.ppermute(piece, "zp", OTHER)
    pieces = (piece, near, lax.ppermute(piece, "c", OTHER), lax.ppermute(near, "c", OTHER))

    rows = a2a(copies(place, own, other, near[:16, :128]), ("zq", "zp", "yh")).reshape(8, 4, 32, 384)
    o_own = o_weight.T
    o_near = lax.ppermute(o_own, "zp", OTHER)

    parts = a2a(project(place, rows, pieces), G + ("zq", "yh")).reshape(8, 16, 2, 1024)
    kv_rows, send = attend(page_table, lengths, parts, k_pool, v_pool, o_near[:16, :128])

    mine = a2a(send.reshape(128, 2, 1536), G + ("zq", "yh")).reshape(256, 1536)
    theirs = lax.ppermute(mine, "c", OTHER)
    out = spread(place, mine, theirs, (o_own, o_near))
    back = a2a(out.reshape(16, 96, 128), G + ("zp",)).reshape(8, 2, 96, 128)
    return (collect(place, back).T, kv_rows)


def solution(mesh):
    parts = Mesh(mesh.devices.reshape(2, 4, 4, 2, 4, 2), G + T)
    in_specs = (
        P(G, T),
        P(G, T),
        P(G, T),
        P(G, T),
        P(G + T, None, None),
        P(G + T, None, None),
        P(G + T, None),
        P(G + T),
    )
    out_specs = (P(G, T), P(G + T, None))
    return jax.shard_map(
        per_device, mesh=parts, in_specs=in_specs, out_specs=out_specs, check_vma=False
    )
```

```python
import jax
import jax.numpy as jnp
from jax import lax
from jax.experimental import pallas as pl
from jax.experimental.pallas import tpu as pltpu
from jax.sharding import Mesh, PartitionSpec as P

D = 12288
HD = 128

eps = 1e-05

G = ("yl", "x")
T = ("zq", "zp", "yh", "c")


def a2a(a, axes):
    return lax.all_to_all(a, axes, split_axis=0, concat_axis=0, tiled=True)


NT = (((1,), (1,)), ((), ()))
VMEM = pl.BlockSpec(memory_space=pltpu.VMEM)
SMEM = pl.BlockSpec(memory_space=pltpu.SMEM)


def in_hbm(a):
    return pltpu.with_memory_space_constraint(a, pltpu.HBM)


def limit(mib):
    return pltpu.CompilerParams(vmem_limit_bytes=mib * 2**20)


def split_kernel(place, hidden, own, other):
    row = lax.broadcasted_iota(jnp.int32, (64, 128), 0)
    col = lax.broadcasted_iota(jnp.int32, (64, 128), 1)
    for out, core in ((own, place[1]), (other, 1 - place[1])):
        goes = ((row // 8) % 4) * 32 + (row // 32) * 16 + ((row // 2) % 4) * 4 + core * 2 + row % 2
        pick = jnp.where(goes == col, 1.0, 0.0).astype(jnp.bfloat16)
        out[...] = lax.dot_general(
            pick, hidden[...], NT, preferred_element_type=jnp.float32
        ).astype(jnp.bfloat16)


def split(place, hidden):
    return pl.pallas_call(
        split_kernel,
        in_specs=[SMEM, VMEM],
        out_specs=[VMEM, VMEM],
        compiler_params=limit(4),
        out_shape=[jax.ShapeDtypeStruct((64, 192), jnp.bfloat16)] * 2,
    )(place, in_hbm(hidden))


def copies_kernel(place, own, other, touch, out):
    del touch
    flip = place[1] == 1
    first = jnp.where(flip, other[...], own[...])
    second = jnp.where(flip, own[...], other[...])
    both = jnp.concatenate([first, second], axis=1)
    for zq in range(4):
        for zp in range(2):
            for y in range(4):
                out[zq * 8 + zp * 4 + y] = both[zp * 32 : zp * 32 + 32]


def copies(place, own, other, touch):
    return pl.pallas_call(
        copies_kernel,
        in_specs=[SMEM] + [VMEM] * 3,
        out_specs=VMEM,
        compiler_params=limit(4),
        out_shape=pltpu.HBM((32, 32, 384), jnp.bfloat16),
    )(place, own, other, touch)


def join_kernel(q, kv, out):
    out[:192] = q[...]
    out[192:] = kv[...]


def join(q, kv):
    return pl.pallas_call(
        join_kernel,
        in_specs=[VMEM] * 2,
        out_specs=VMEM,
        compiler_params=limit(4),
        out_shape=jax.ShapeDtypeStruct((224, 1536), jnp.bfloat16),
    )(in_hbm(q), in_hbm(kv))


def project_kernel(place, rows, own, near, own_other, near_other, out, weight, sem):
    zp, core = place[0], place[1]
    fetches = []
    for k, (piece, z, c) in enumerate(
        (
            (own, zp, core),
            (near, 1 - zp, core),
            (own_other, zp, 1 - core),
            (near_other, 1 - zp, 1 - core),
        )
    ):
        at = z * 2 + c
        q_rows = pl.ds(pl.multiple_of(at * 192, 64), 192)
        kv_rows = pl.ds(pl.multiple_of(768 + at * 32, 32), 32)
        fetches.append(pltpu.make_async_copy(piece.at[:192], weight.at[q_rows], sem.at[2 * k]))
        fetches.append(
            pltpu.make_async_copy(piece.at[192:], weight.at[kv_rows], sem.at[2 * k + 1])
        )
    for fetch in fetches:
        fetch.start()
    lane = lax.broadcasted_iota(jnp.int32, (128, 128), 1)
    for half in range(2):
        wide = 0
        for y in range(4):
            a = rows[half * 4 : half * 4 + 4, y].reshape(128, 384).astype(jnp.float32)
            a = a * a
            wide += a[:, :128] + a[:, 128:256] + a[:, 256:]
        sums = jnp.sum(wide, axis=1, keepdims=True)
        high = sums.astype(jnp.bfloat16).astype(jnp.float32)
        extra = jnp.where(lane == 0, high, jnp.where(lane == 1, sums - high, 0.0))
        out[half * 128 : half * 128 + 128, 896:] = extra.astype(jnp.bfloat16)
    for fetch in fetches:
        fetch.wait()
    total = 0
    for y in range(4):
        total += lax.dot_general(
            rows[:, y].reshape(256, 384),
            weight[:, y * 384 : y * 384 + 384],
            NT,
            preferred_element_type=jnp.float32,
        )
    out[:, :896] = total.astype(jnp.bfloat16)


def project(place, rows, pieces):
    return pl.pallas_call(
        project_kernel,
        in_specs=[SMEM, VMEM] + [pl.BlockSpec(memory_space=pl.ANY)] * 4,
        out_specs=VMEM,
        out_shape=pltpu.HBM((256, 1024), jnp.bfloat16),
        scratch_shapes=[pltpu.VMEM((896, 1536), jnp.bfloat16), pltpu.SemaphoreType.DMA((8,))],
        compiler_params=limit(16),
        cost_estimate=pl.CostEstimate(
            flops=2 * 256 * 1536 * 896, bytes_accessed=4 * 2**20, transcendentals=0
        ),
    )(place, rows, *(in_hbm(piece) for piece in pieces))


def add_kernel(parts, out):
    total = jnp.sum(parts[...].astype(jnp.float32), axis=0)
    squares = jnp.sum(total[:, 896:], axis=1, keepdims=True)
    normed = total[:, :896] * lax.rsqrt(squares / D + eps)
    for r in range(8):
        out[r] = normed[2 * r : 2 * r + 2].astype(jnp.bfloat16)


def add(parts):
    return pl.pallas_call(
        add_kernel,
        grid=(2,),
        in_specs=[
            pl.BlockSpec((8, 16, 1024), lambda i: (0, i, 0)),
        ],
        out_specs=pl.BlockSpec((8, 2, 896), lambda i: (i, 0, 0)),
        compiler_params=limit(4),
        out_shape=pltpu.HBM((16, 2, 896), jnp.bfloat16),
    )(parts)


def attend_kernel(table, lengths, parts, k_pool, v_pool, first, second, new_kv, send, query, mixed, v_held, sem, v_sem):
    del first, second
    fetch = pltpu.make_async_copy(v_pool, v_held, v_sem)
    fetch.start()
    row = lax.broadcasted_iota(jnp.int32, (24, 768), 0) % 2
    lane = lax.broadcasted_iota(jnp.int32, (1, 768), 1)
    masks = []
    for r in range(2):
        mask = jnp.zeros((1, 768), jnp.int32)
        for page in range(12):
            start = table[r, page] * 32
            end = start + jnp.clip(lengths[r] - page * 32, 0, 32)
            mask = jnp.where((lane >= start) & (lane < end), 1, mask)
        masks.append(mask)
    valid = jnp.where(row == 0, masks[0], masks[1]) == 1

    for z in range(8):
        zq, zp = z // 2, z % 2
        for y in range(4):
            for k in range(3):
                at, h = zp * 384 + k * 128, y * 3 + k
                query[z, 2 * h : 2 * h + 2, :] = parts[zq * 4 + y, :, at : at + 128].astype(
                    jnp.float32
                )
    fresh = []
    for z in range(8):
        at = 768 + (z % 2) * 64
        for y in range(0, 4, 2):
            pair = [
                parts[(z // 2) * 4 + y + k, :, at : at + 64].astype(jnp.float32) for k in range(2)
            ]
            fresh.append(jnp.concatenate(pair, axis=1))
            to = z * 256 + y * 64
            new_kv[:, to : to + 128] = fresh[-1].astype(jnp.bfloat16)

    scale = 1.0 / jnp.sqrt(jnp.float32(HD))
    odd = lax.broadcasted_iota(jnp.int32, (24, 128), 0) % 2 == 1
    found = []
    for g in range(8):
        keys = k_pool[:, :, g * 128 : g * 128 + 128].reshape(768, 128)
        own_key = jnp.where(odd, fresh[g][1:2], fresh[g][0:1])
        q = query[g]
        scores = lax.dot_general(
            q.astype(jnp.bfloat16), keys, NT, preferred_element_type=jnp.float32
        )
        scores = jnp.where(valid, scores * scale, jnp.float32(-1e30))
        own = jnp.sum(q * own_key, axis=1, keepdims=True) * scale
        top = jnp.maximum(jnp.max(scores, axis=1, keepdims=True), own)
        scores = jnp.exp(scores - top)
        own = jnp.exp(own - top)
        total = jnp.sum(scores, axis=1, keepdims=True) + own
        weights = (scores / total).astype(jnp.bfloat16)
        found.append((weights, (own / total).astype(jnp.bfloat16).astype(jnp.float32)))
    fetch.wait()
    for g, (weights, own) in enumerate(found):
        values = v_held[:, :, g * 128 : g * 128 + 128].reshape(768, 128)
        own_value = jnp.where(odd, fresh[8 + g][1:2], fresh[8 + g][0:1])
        out = lax.dot_general(
            weights, values, (((1,), (0,)), ((), ())), preferred_element_type=jnp.float32
        )
        out = out + own * own_value
        for h in range(12):
            mixed[g, :, h * 128 : h * 128 + 128] = out[2 * h : 2 * h + 2].astype(jnp.bfloat16)
    copies = [pltpu.make_async_copy(mixed, send.at[:, k], sem.at[k]) for k in range(16)]
    for copy in copies:
        copy.start()
    for copy in copies:
        copy.wait()


def attend(table, lengths, parts, k_pool, v_pool, first, second):
    return pl.pallas_call(
        attend_kernel,
        in_specs=[SMEM] * 2 + [VMEM] * 2 + [pl.BlockSpec(memory_space=pl.ANY)] + [VMEM] * 2,
        out_specs=[VMEM, pl.BlockSpec(memory_space=pl.ANY)],
        out_shape=[
            jax.ShapeDtypeStruct((2, 2048), jnp.bfloat16),
            pltpu.HBM((8, 16, 2, 1536), jnp.bfloat16),
        ],
        scratch_shapes=[
            pltpu.VMEM((8, 24, 128), jnp.float32),
            pltpu.VMEM((8, 2, 1536), jnp.bfloat16),
            pltpu.VMEM((24, 32, 1024), jnp.bfloat16),
            pltpu.SemaphoreType.DMA((16,)),
            pltpu.SemaphoreType.DMA,
        ],
        compiler_params=limit(16),
    )(table, lengths, parts, k_pool, in_hbm(v_pool), first, second)


def spread_kernel(place, rows, *refs):
    zp, core = place[0], place[1]
    out = refs[4]
    for k in range(4):
        weight = refs[k][...]
        z = zp if k % 2 == 0 else 1 - zp
        c = core if k < 2 else 1 - core
        part = lax.dot_general(rows[...], weight, NT, preferred_element_type=jnp.float32)
        part = part.astype(jnp.bfloat16)
        for g in range(8):
            at = g * 32
            out[g, z * 2 + c, 0:32, :] = part[at : at + 32, :128]
            out[g, z * 2 + c, 32:48, :] = jnp.concatenate(
                [part[at : at + 16, 128:], part[at + 16 : at + 32, 128:]], axis=1
            )


def spread(place, rows, pieces):
    return pl.pallas_call(
        spread_kernel,
        in_specs=[SMEM] + [VMEM] * 5,
        out_specs=VMEM,
        out_shape=jax.ShapeDtypeStruct((8, 4, 48, 128), jnp.bfloat16),
        compiler_params=limit(16),
        cost_estimate=pl.CostEstimate(
            flops=2 * 256 * 1536 * 768, bytes_accessed=4 * 2**20, transcendentals=0
        ),
    )(place, rows, *pieces)


def collect_kernel(parts, out):
    total = jnp.sum(parts[...].astype(jnp.float32), axis=0).astype(jnp.bfloat16)
    rows = []
    for k in range(4):
        last = jnp.concatenate([total[k, 32:48, :64], total[k, 32:48, 64:]], axis=0)
        rows.append(jnp.concatenate([total[k, 0:32], last], axis=1))
    rows = jnp.concatenate(rows, axis=0)
    at = lax.broadcasted_iota(jnp.int32, (128, 128), 0)
    to = lax.broadcasted_iota(jnp.int32, (128, 128), 1)
    goes = ((at // 8) % 4) * 32 + (at // 64) * 16 + ((at // 2) % 4) * 4 + ((at // 32) % 2) * 2 + at % 2
    pick = jnp.where(goes == to, 1.0, 0.0).astype(jnp.bfloat16)
    out[...] = lax.dot_general(
        rows, pick, (((0,), (0,)), ((), ())), preferred_element_type=jnp.float32
    ).astype(jnp.bfloat16)


def collect(parts):
    return pl.pallas_call(
        collect_kernel,
        in_specs=[VMEM],
        out_specs=VMEM,
        compiler_params=limit(4),
        out_shape=jax.ShapeDtypeStruct((192, 128), jnp.bfloat16),
    )(parts)


OTHER = [(0, 1), (1, 0)]


def per_device(hidden, q_weight, kv_weight, o_weight, k_pool, v_pool, page_table, lengths):
    place = jnp.stack([lax.axis_index("zp"), lax.axis_index("c")])
    place = place.astype(jnp.int32)

    own = join(q_weight.T, kv_weight.T)
    near = lax.ppermute(own, "zp", OTHER)
    pieces = (own, near, lax.ppermute(own, "c", OTHER), lax.ppermute(near, "c", OTHER))
    o_own = o_weight.T
    o_near = lax.ppermute(o_own, "zp", OTHER)
    o_pieces = (o_own, o_near, lax.ppermute(o_own, "c", OTHER), lax.ppermute(o_near, "c", OTHER))

    rows = [
        lax.ppermute(
            part,
            G + ("zq", "zp", "c"),
            [
                ((g * 8 + z) * 2 + c, (z * 8 + g) * 2 + (c ^ flip))
                for g in range(8)
                for z in range(8)
                for c in range(2)
            ],
        )
        for flip, part in enumerate(split(place, hidden.T))
    ]
    rows = a2a(copies(place, *rows, near[:16, :128]), ("zq", "zp", "yh")).reshape(8, 4, 32, 384)

    parts = a2a(project(place, rows, pieces).reshape(8, 32, 1024), G)
    parts = a2a(add(parts), ("zq", "yh"))
    first, second = (piece[:16, :128] for piece in o_pieces[2:])
    kv_rows, send = attend(page_table, lengths, parts, k_pool, v_pool, first, second)

    mine = a2a(send.reshape(128, 2, 1536), G + ("zq", "yh")).reshape(256, 1536)
    out = spread(place, mine, o_pieces)
    back = a2a(out.reshape(32, 48, 128), G + ("zp", "c")).reshape(8, 4, 48, 128)
    return (collect(back).T, kv_rows)


def solution(mesh):
    parts = Mesh(mesh.devices.reshape(2, 4, 4, 2, 4, 2), G + T)
    in_specs = (
        P(G, T),
        P(G, T),
        P(G, T),
        P(G, T),
        P(G + T, None, None),
        P(G + T, None, None),
        P(G + T, None),
        P(G + T),
    )
    out_specs = (P(G, T), P(G + T, None))
    return jax.shard_map(
        per_device, mesh=parts, in_specs=in_specs, out_specs=out_specs, check_vma=False
    )
```

```python
import jax
import jax.numpy as jnp
from jax import lax
from jax.experimental import pallas as pl
from jax.experimental.pallas import tpu as pltpu
from jax.sharding import Mesh, PartitionSpec as P

D = 12288
HD = 128

eps = 1e-05

G = ("yl", "x")
T = ("zq", "zp", "yh", "c")


def a2a(a, axes):
    return lax.all_to_all(a, axes, split_axis=0, concat_axis=0, tiled=True)


NT = (((1,), (1,)), ((), ()))
VMEM = pl.BlockSpec(memory_space=pltpu.VMEM)
SMEM = pl.BlockSpec(memory_space=pltpu.SMEM)


def in_hbm(a):
    return pltpu.with_memory_space_constraint(a, pltpu.HBM)


def limit(mib):
    return pltpu.CompilerParams(vmem_limit_bytes=mib * 2**20)


def split_kernel(place, hidden, own, other):
    row = lax.broadcasted_iota(jnp.int32, (64, 128), 0)
    col = lax.broadcasted_iota(jnp.int32, (64, 128), 1)
    for out, core in ((own, place[1]), (other, 1 - place[1])):
        goes = ((row // 8) % 4) * 32 + (row // 32) * 16 + ((row // 2) % 4) * 4 + core * 2 + row % 2
        pick = jnp.where(goes == col, 1.0, 0.0).astype(jnp.bfloat16)
        out[...] = lax.dot_general(
            pick, hidden[...], NT, preferred_element_type=jnp.float32
        ).astype(jnp.bfloat16)


def split(place, hidden):
    return pl.pallas_call(
        split_kernel,
        in_specs=[SMEM, VMEM],
        out_specs=[VMEM, VMEM],
        compiler_params=limit(4),
        out_shape=[jax.ShapeDtypeStruct((64, 192), jnp.bfloat16)] * 2,
    )(place, in_hbm(hidden))


def copies_kernel(place, own, other, touch, out):
    del touch
    flip = place[1] == 1
    first = jnp.where(flip, other[...], own[...])
    second = jnp.where(flip, own[...], other[...])
    both = jnp.concatenate([first, second], axis=1)
    for zq in range(4):
        for zp in range(2):
            for y in range(4):
                out[zq * 8 + zp * 4 + y] = both[zp * 32 : zp * 32 + 32]


def copies(place, own, other, touch):
    return pl.pallas_call(
        copies_kernel,
        in_specs=[SMEM] + [VMEM] * 3,
        out_specs=VMEM,
        compiler_params=limit(4),
        out_shape=pltpu.HBM((32, 32, 384), jnp.bfloat16),
    )(place, own, other, touch)


def join_kernel(q, kv, out):
    out[:192] = q[...]
    out[192:] = kv[...]


def join(q, kv):
    return pl.pallas_call(
        join_kernel,
        in_specs=[VMEM] * 2,
        out_specs=VMEM,
        compiler_params=limit(4),
        out_shape=jax.ShapeDtypeStruct((224, 1536), jnp.bfloat16),
    )(in_hbm(q), in_hbm(kv))


def project_kernel(place, rows, own, near, own_other, near_other, out, weight, sem):
    zp, core = place[0], place[1]
    fetches = []
    for k, (piece, z, c) in enumerate(
        (
            (own, zp, core),
            (near, 1 - zp, core),
            (own_other, zp, 1 - core),
            (near_other, 1 - zp, 1 - core),
        )
    ):
        at = z * 2 + c
        q_rows = pl.ds(pl.multiple_of(at * 192, 64), 192)
        kv_rows = pl.ds(pl.multiple_of(768 + at * 32, 32), 32)
        fetches.append(pltpu.make_async_copy(piece.at[:192], weight.at[q_rows], sem.at[2 * k]))
        fetches.append(
            pltpu.make_async_copy(piece.at[192:], weight.at[kv_rows], sem.at[2 * k + 1])
        )
    for fetch in fetches:
        fetch.start()
    lane = lax.broadcasted_iota(jnp.int32, (128, 128), 1)
    extras = []
    for half in range(2):
        wide = 0
        for y in range(4):
            a = rows[half * 4 : half * 4 + 4, y].reshape(128, 384).astype(jnp.float32)
            a = a * a
            wide += a[:, :128] + a[:, 128:256] + a[:, 256:]
        sums = jnp.sum(wide, axis=1, keepdims=True)
        high = sums.astype(jnp.bfloat16).astype(jnp.float32)
        extras.append(jnp.where(lane == 0, high, jnp.where(lane == 1, sums - high, 0.0)))
    for fetch in fetches:
        fetch.wait()
    for half in range(2):
        total = 0
        for y in range(4):
            total += lax.dot_general(
                rows[half * 4 : half * 4 + 4, y].reshape(128, 384),
                weight[:, y * 384 : y * 384 + 384],
                NT,
                preferred_element_type=jnp.float32,
            )
        for r in range(64):
            at = slice(2 * r, 2 * r + 2)
            out[half * 64 + r, :, :896] = total[at].astype(jnp.bfloat16)
            out[half * 64 + r, :, 896:] = extras[half][at].astype(jnp.bfloat16)


def project(place, rows, pieces):
    return pl.pallas_call(
        project_kernel,
        in_specs=[SMEM, VMEM] + [pl.BlockSpec(memory_space=pl.ANY)] * 4,
        out_specs=VMEM,
        out_shape=pltpu.HBM((128, 2, 1024), jnp.bfloat16),
        scratch_shapes=[pltpu.VMEM((896, 1536), jnp.bfloat16), pltpu.SemaphoreType.DMA((8,))],
        compiler_params=limit(16),
        cost_estimate=pl.CostEstimate(
            flops=2 * 256 * 1536 * 896, bytes_accessed=4 * 2**20, transcendentals=0
        ),
    )(place, rows, *(in_hbm(piece) for piece in pieces))


def attend_kernel(table, lengths, parts, k_pool, v_pool, first, second, new_kv, send, query, mixed, v_held, sem, v_sem):
    del first, second
    fetch = pltpu.make_async_copy(v_pool, v_held, v_sem)
    fetch.start()
    row = lax.broadcasted_iota(jnp.int32, (24, 768), 0) % 2
    lane = lax.broadcasted_iota(jnp.int32, (1, 768), 1)
    masks = []
    for r in range(2):
        mask = jnp.zeros((1, 768), jnp.int32)
        for page in range(12):
            start = table[r, page] * 32
            end = start + jnp.clip(lengths[r] - page * 32, 0, 32)
            mask = jnp.where((lane >= start) & (lane < end), 1, mask)
        masks.append(mask)
    valid = jnp.where(row == 0, masks[0], masks[1]) == 1

    normed = []
    for k in range(16):
        total = jnp.sum(parts[:, k].astype(jnp.float32), axis=0)
        if k == 0:
            squares = jnp.sum(total[:, 896:], axis=1, keepdims=True)
            inv_rms = lax.rsqrt(squares / D + eps)
        normed.append((total[:, :896] * inv_rms).astype(jnp.bfloat16).astype(jnp.float32))
    for z in range(8):
        zq, zp = z // 2, z % 2
        for y in range(4):
            for k in range(3):
                at, h = zp * 384 + k * 128, y * 3 + k
                query[z, 2 * h : 2 * h + 2, :] = normed[zq * 4 + y][:, at : at + 128]
    fresh = []
    for z in range(8):
        at = 768 + (z % 2) * 64
        for y in range(0, 4, 2):
            pair = [normed[(z // 2) * 4 + y + k][:, at : at + 64] for k in range(2)]
            fresh.append(jnp.concatenate(pair, axis=1))
            to = z * 256 + y * 64
            new_kv[:, to : to + 128] = fresh[-1].astype(jnp.bfloat16)

    scale = 1.0 / jnp.sqrt(jnp.float32(HD))
    odd = lax.broadcasted_iota(jnp.int32, (24, 128), 0) % 2 == 1
    found = []
    for g in range(8):
        keys = k_pool[:, :, g * 128 : g * 128 + 128].reshape(768, 128)
        own_key = jnp.where(odd, fresh[g][1:2], fresh[g][0:1])
        q = query[g]
        scores = lax.dot_general(
            q.astype(jnp.bfloat16), keys, NT, preferred_element_type=jnp.float32
        )
        scores = jnp.where(valid, scores * scale, jnp.float32(-1e30))
        own = jnp.sum(q * own_key, axis=1, keepdims=True) * scale
        top = jnp.maximum(jnp.max(scores, axis=1, keepdims=True), own)
        scores = jnp.exp(scores - top)
        own = jnp.exp(own - top)
        total = jnp.sum(scores, axis=1, keepdims=True) + own
        weights = (scores / total).astype(jnp.bfloat16)
        found.append((weights, (own / total).astype(jnp.bfloat16).astype(jnp.float32)))
    fetch.wait()
    copies = []
    for g, (weights, own) in enumerate(found):
        values = v_held[:, :, g * 128 : g * 128 + 128].reshape(768, 128)
        own_value = jnp.where(odd, fresh[8 + g][1:2], fresh[8 + g][0:1])
        out = lax.dot_general(
            weights, values, (((1,), (0,)), ((), ())), preferred_element_type=jnp.float32
        )
        out = out + own * own_value
        for h in range(12):
            mixed[g, :, h * 128 : h * 128 + 128] = out[2 * h : 2 * h + 2].astype(jnp.bfloat16)
        if g % 4 == 3:
            part = pl.ds(g - 3, 4)
            for k in range(16):
                copies.append(
                    pltpu.make_async_copy(
                        mixed.at[part], send.at[part, k], sem.at[g // 4 * 16 + k]
                    )
                )
                copies[-1].start()
    for copy in copies:
        copy.wait()


def attend(table, lengths, parts, k_pool, v_pool, first, second):
    return pl.pallas_call(
        attend_kernel,
        in_specs=[SMEM] * 2 + [VMEM] * 2 + [pl.BlockSpec(memory_space=pl.ANY)] + [VMEM] * 2,
        out_specs=[VMEM, pl.BlockSpec(memory_space=pl.ANY)],
        out_shape=[
            jax.ShapeDtypeStruct((2, 2048), jnp.bfloat16),
            pltpu.HBM((8, 16, 2, 1536), jnp.bfloat16),
        ],
        scratch_shapes=[
            pltpu.VMEM((8, 24, 128), jnp.float32),
            pltpu.VMEM((8, 2, 1536), jnp.bfloat16),
            pltpu.VMEM((24, 32, 1024), jnp.bfloat16),
            pltpu.SemaphoreType.DMA((32,)),
            pltpu.SemaphoreType.DMA,
        ],
        compiler_params=limit(16),
    )(table, lengths, parts, k_pool, in_hbm(v_pool), first, second)


def spread_kernel(place, rows, *refs):
    zp, core = place[0], place[1]
    out = refs[4]
    for k in range(4):
        weight = refs[k][...]
        z = zp if k % 2 == 0 else 1 - zp
        c = core if k < 2 else 1 - core
        part = lax.dot_general(rows[...], weight, NT, preferred_element_type=jnp.float32)
        part = part.astype(jnp.bfloat16)
        for g in range(8):
            at = g * 32
            out[g, z * 2 + c, 0:32, :] = part[at : at + 32, :128]
            out[g, z * 2 + c, 32:48, :] = jnp.concatenate(
                [part[at : at + 16, 128:], part[at + 16 : at + 32, 128:]], axis=1
            )


def spread(place, rows, pieces):
    return pl.pallas_call(
        spread_kernel,
        in_specs=[SMEM] + [VMEM] * 5,
        out_specs=VMEM,
        out_shape=jax.ShapeDtypeStruct((8, 4, 48, 128), jnp.bfloat16),
        compiler_params=limit(16),
        cost_estimate=pl.CostEstimate(
            flops=2 * 256 * 1536 * 768, bytes_accessed=4 * 2**20, transcendentals=0
        ),
    )(place, rows, *pieces)


def collect_kernel(parts, out):
    total = jnp.sum(parts[...].astype(jnp.float32), axis=0).astype(jnp.bfloat16)
    rows = []
    for k in range(4):
        last = jnp.concatenate([total[k, 32:48, :64], total[k, 32:48, 64:]], axis=0)
        rows.append(jnp.concatenate([total[k, 0:32], last], axis=1))
    rows = jnp.concatenate(rows, axis=0)
    at = lax.broadcasted_iota(jnp.int32, (128, 128), 0)
    to = lax.broadcasted_iota(jnp.int32, (128, 128), 1)
    goes = ((at // 8) % 4) * 32 + (at // 64) * 16 + ((at // 2) % 4) * 4 + ((at // 32) % 2) * 2 + at % 2
    pick = jnp.where(goes == to, 1.0, 0.0).astype(jnp.bfloat16)
    out[...] = lax.dot_general(
        rows, pick, (((0,), (0,)), ((), ())), preferred_element_type=jnp.float32
    ).astype(jnp.bfloat16)


def collect(parts):
    return pl.pallas_call(
        collect_kernel,
        in_specs=[VMEM],
        out_specs=VMEM,
        compiler_params=limit(4),
        out_shape=jax.ShapeDtypeStruct((192, 128), jnp.bfloat16),
    )(parts)


OTHER = [(0, 1), (1, 0)]


def per_device(hidden, q_weight, kv_weight, o_weight, k_pool, v_pool, page_table, lengths):
    place = jnp.stack([lax.axis_index("zp"), lax.axis_index("c")])
    place = place.astype(jnp.int32)

    own = join(q_weight.T, kv_weight.T)
    near = lax.ppermute(own, "zp", OTHER)
    pieces = (own, near, lax.ppermute(own, "c", OTHER), lax.ppermute(near, "c", OTHER))
    o_own = o_weight.T
    o_near = lax.ppermute(o_own, "zp", OTHER)
    o_pieces = (o_own, o_near, lax.ppermute(o_own, "c", OTHER), lax.ppermute(o_near, "c", OTHER))

    rows = [
        lax.ppermute(
            part,
            G + ("zq", "zp", "c"),
            [
                ((g * 8 + z) * 2 + c, (z * 8 + g) * 2 + (c ^ flip))
                for g in range(8)
                for z in range(8)
                for c in range(2)
            ],
        )
        for flip, part in enumerate(split(place, hidden.T))
    ]
    rows = a2a(copies(place, *rows, near[:16, :128]), ("zq", "zp", "yh")).reshape(8, 4, 32, 384)

    parts = a2a(project(place, rows, pieces), G + ("zq", "yh")).reshape(8, 16, 2, 1024)
    first, second = (piece[:16, :128] for piece in o_pieces[2:])
    kv_rows, send = attend(page_table, lengths, parts, k_pool, v_pool, first, second)

    mine = a2a(send.reshape(128, 2, 1536), G + ("zq", "yh")).reshape(256, 1536)
    out = spread(place, mine, o_pieces)
    back = a2a(out.reshape(32, 48, 128), G + ("zp", "c")).reshape(8, 4, 48, 128)
    return (collect(back).T, kv_rows)


def solution(mesh):
    parts = Mesh(mesh.devices.reshape(2, 4, 4, 2, 4, 2), G + T)
    in_specs = (
        P(G, T),
        P(G, T),
        P(G, T),
        P(G, T),
        P(G + T, None, None),
        P(G + T, None, None),
        P(G + T, None),
        P(G + T),
    )
    out_specs = (P(G, T), P(G + T, None))
    return jax.shard_map(
        per_device, mesh=parts, in_specs=in_specs, out_specs=out_specs, check_vma=False
    )
```

```python
import jax
import jax.numpy as jnp
from jax import lax
from jax.experimental import pallas as pl
from jax.experimental.pallas import tpu as pltpu
from jax.sharding import Mesh, PartitionSpec as P

D = 12288
HD = 128

eps = 1e-05

G = ("yl", "x")
T = ("zq", "zp", "yh", "c")


def a2a(a, axes):
    return lax.all_to_all(a, axes, split_axis=0, concat_axis=0, tiled=True)


NT = (((1,), (1,)), ((), ()))
VMEM = pl.BlockSpec(memory_space=pltpu.VMEM)
SMEM = pl.BlockSpec(memory_space=pltpu.SMEM)


def in_hbm(a):
    return pltpu.with_memory_space_constraint(a, pltpu.HBM)


def limit(mib):
    return pltpu.CompilerParams(vmem_limit_bytes=mib * 2**20)


def split_kernel(place, hidden, own, other):
    row = lax.broadcasted_iota(jnp.int32, (64, 128), 0)
    col = lax.broadcasted_iota(jnp.int32, (64, 128), 1)
    for out, core in ((own, place[1]), (other, 1 - place[1])):
        goes = ((row // 8) % 4) * 32 + (row // 32) * 16 + ((row // 2) % 4) * 4 + core * 2 + row % 2
        pick = jnp.where(goes == col, 1.0, 0.0).astype(jnp.bfloat16)
        out[...] = lax.dot_general(
            pick, hidden[...], NT, preferred_element_type=jnp.float32
        ).astype(jnp.bfloat16)


def split(place, hidden):
    return pl.pallas_call(
        split_kernel,
        in_specs=[SMEM, VMEM],
        out_specs=[VMEM, VMEM],
        compiler_params=limit(4),
        out_shape=[jax.ShapeDtypeStruct((64, 192), jnp.bfloat16)] * 2,
    )(place, in_hbm(hidden))


def copies_kernel(place, own, other, first, second, out):
    del first, second
    flip = place[1] == 1
    first = jnp.where(flip, other[...], own[...])
    second = jnp.where(flip, own[...], other[...])
    both = jnp.concatenate([first, second], axis=1)
    for zq in range(4):
        for zp in range(2):
            for y in range(4):
                out[zq * 8 + zp * 4 + y] = both[zp * 32 : zp * 32 + 32]


def copies(place, own, other, first, second):
    return pl.pallas_call(
        copies_kernel,
        in_specs=[SMEM] + [VMEM] * 4,
        out_specs=VMEM,
        compiler_params=limit(4),
        out_shape=pltpu.HBM((32, 32, 384), jnp.bfloat16),
    )(place, own, other, first, second)


def project_kernel(place, rows, *refs):
    zp, core = place[0], place[1]
    out, weight, sem = refs[8:]
    fetches = []
    for y in range(4):
        part = slice(y * 384, y * 384 + 384)
        for k, (z, c) in enumerate(
            ((zp, core), (1 - zp, core), (zp, 1 - core), (1 - zp, 1 - core))
        ):
            at = z * 2 + c
            q_rows = pl.ds(pl.multiple_of(at * 192, 64), 192)
            kv_rows = pl.ds(pl.multiple_of(768 + at * 32, 32), 32)
            for j, to in enumerate((q_rows, kv_rows)):
                fetches.append(
                    pltpu.make_async_copy(
                        refs[2 * k + j].at[:, part],
                        weight.at[to, part],
                        sem.at[y * 8 + 2 * k + j],
                    )
                )
                fetches[-1].start()
    lane = lax.broadcasted_iota(jnp.int32, (128, 128), 1)
    extras = []
    for half in range(2):
        wide = 0
        for y in range(4):
            a = rows[half * 4 : half * 4 + 4, y].reshape(128, 384).astype(jnp.float32)
            a = a * a
            wide += a[:, :128] + a[:, 128:256] + a[:, 256:]
        sums = jnp.sum(wide, axis=1, keepdims=True)
        high = sums.astype(jnp.bfloat16).astype(jnp.float32)
        extras.append(jnp.where(lane == 0, high, jnp.where(lane == 1, sums - high, 0.0)))
    total = [0, 0]
    for y in range(4):
        for fetch in fetches[y * 8 : y * 8 + 8]:
            fetch.wait()
        for half in range(2):
            total[half] += lax.dot_general(
                rows[half * 4 : half * 4 + 4, y].reshape(128, 384),
                weight[:, y * 384 : y * 384 + 384],
                NT,
                preferred_element_type=jnp.float32,
            )
    for half in range(2):
        for r in range(64):
            at = slice(2 * r, 2 * r + 2)
            out[half * 64 + r, :, :896] = total[half][at].astype(jnp.bfloat16)
            out[half * 64 + r, :, 896:] = extras[half][at].astype(jnp.bfloat16)


def project(place, rows, pieces):
    return pl.pallas_call(
        project_kernel,
        in_specs=[SMEM, VMEM] + [pl.BlockSpec(memory_space=pl.ANY)] * 8,
        out_specs=VMEM,
        out_shape=pltpu.HBM((128, 2, 1024), jnp.bfloat16),
        scratch_shapes=[pltpu.VMEM((896, 1536), jnp.bfloat16), pltpu.SemaphoreType.DMA((32,))],
        compiler_params=limit(16),
        cost_estimate=pl.CostEstimate(
            flops=2 * 256 * 1536 * 896, bytes_accessed=4 * 2**20, transcendentals=0
        ),
    )(place, rows, *(in_hbm(piece) for piece in pieces))


def attend_kernel(table, lengths, parts, k_pool, v_pool, first, second, new_kv, send, query, mixed, v_held, sem, v_sem):
    del first, second
    fetch = pltpu.make_async_copy(v_pool, v_held, v_sem)
    fetch.start()
    row = lax.broadcasted_iota(jnp.int32, (24, 768), 0) % 2
    lane = lax.broadcasted_iota(jnp.int32, (1, 768), 1)
    masks = []
    for r in range(2):
        mask = jnp.zeros((1, 768), jnp.int32)
        for page in range(12):
            start = table[r, page] * 32
            end = start + jnp.clip(lengths[r] - page * 32, 0, 32)
            mask = jnp.where((lane >= start) & (lane < end), 1, mask)
        masks.append(mask)
    valid = jnp.where(row == 0, masks[0], masks[1]) == 1

    normed = []
    for k in range(16):
        total = jnp.sum(parts[:, k].astype(jnp.float32), axis=0)
        if k == 0:
            squares = jnp.sum(total[:, 896:], axis=1, keepdims=True)
            inv_rms = lax.rsqrt(squares / D + eps)
        normed.append((total[:, :896] * inv_rms).astype(jnp.bfloat16).astype(jnp.float32))
    for z in range(8):
        zq, zp = z // 2, z % 2
        for y in range(4):
            for k in range(3):
                at, h = zp * 384 + k * 128, y * 3 + k
                query[z, 2 * h : 2 * h + 2, :] = normed[zq * 4 + y][:, at : at + 128]
    fresh = []
    for z in range(8):
        at = 768 + (z % 2) * 64
        for y in range(0, 4, 2):
            pair = [normed[(z // 2) * 4 + y + k][:, at : at + 64] for k in range(2)]
            fresh.append(jnp.concatenate(pair, axis=1))
            to = z * 256 + y * 64
            new_kv[:, to : to + 128] = fresh[-1].astype(jnp.bfloat16)

    scale = 1.0 / jnp.sqrt(jnp.float32(HD))
    odd = lax.broadcasted_iota(jnp.int32, (24, 128), 0) % 2 == 1
    found = []
    for g in range(8):
        keys = k_pool[:, :, g * 128 : g * 128 + 128].reshape(768, 128)
        own_key = jnp.where(odd, fresh[g][1:2], fresh[g][0:1])
        q = query[g]
        scores = lax.dot_general(
            q.astype(jnp.bfloat16), keys, NT, preferred_element_type=jnp.float32
        )
        scores = jnp.where(valid, scores * scale, jnp.float32(-1e30))
        own = jnp.sum(q * own_key, axis=1, keepdims=True) * scale
        top = jnp.maximum(jnp.max(scores, axis=1, keepdims=True), own)
        scores = jnp.exp(scores - top)
        own = jnp.exp(own - top)
        total = jnp.sum(scores, axis=1, keepdims=True) + own
        weights = (scores / total).astype(jnp.bfloat16)
        found.append((weights, (own / total).astype(jnp.bfloat16).astype(jnp.float32)))
    fetch.wait()
    copies = []
    for g, (weights, own) in enumerate(found):
        values = v_held[:, :, g * 128 : g * 128 + 128].reshape(768, 128)
        own_value = jnp.where(odd, fresh[8 + g][1:2], fresh[8 + g][0:1])
        out = lax.dot_general(
            weights, values, (((1,), (0,)), ((), ())), preferred_element_type=jnp.float32
        )
        out = out + own * own_value
        for h in range(12):
            mixed[g, :, h * 128 : h * 128 + 128] = out[2 * h : 2 * h + 2].astype(jnp.bfloat16)
        if g % 4 == 3:
            part = pl.ds(g - 3, 4)
            for k in range(16):
                copies.append(
                    pltpu.make_async_copy(
                        mixed.at[part], send.at[part, k], sem.at[g // 4 * 16 + k]
                    )
                )
                copies[-1].start()
    for copy in copies:
        copy.wait()


def attend(table, lengths, parts, k_pool, v_pool, first, second):
    return pl.pallas_call(
        attend_kernel,
        in_specs=[SMEM] * 2 + [VMEM] * 2 + [pl.BlockSpec(memory_space=pl.ANY)] + [VMEM] * 2,
        out_specs=[VMEM, pl.BlockSpec(memory_space=pl.ANY)],
        out_shape=[
            jax.ShapeDtypeStruct((2, 2048), jnp.bfloat16),
            pltpu.HBM((8, 16, 2, 1536), jnp.bfloat16),
        ],
        scratch_shapes=[
            pltpu.VMEM((8, 24, 128), jnp.float32),
            pltpu.VMEM((8, 2, 1536), jnp.bfloat16),
            pltpu.VMEM((24, 32, 1024), jnp.bfloat16),
            pltpu.SemaphoreType.DMA((32,)),
            pltpu.SemaphoreType.DMA,
        ],
        compiler_params=limit(16),
    )(table, lengths, parts, k_pool, in_hbm(v_pool), first, second)


def spread_kernel(place, rows, *refs):
    zp, core = place[0], place[1]
    out = refs[4]
    for k in range(4):
        weight = refs[k][...]
        z = zp if k % 2 == 0 else 1 - zp
        c = core if k < 2 else 1 - core
        part = lax.dot_general(rows[...], weight, NT, preferred_element_type=jnp.float32)
        part = part.astype(jnp.bfloat16)
        for g in range(8):
            at = g * 32
            out[g, z * 2 + c, 0:32, :] = part[at : at + 32, :128]
            out[g, z * 2 + c, 32:48, :] = jnp.concatenate(
                [part[at : at + 16, 128:], part[at + 16 : at + 32, 128:]], axis=1
            )


def spread(place, rows, pieces):
    return pl.pallas_call(
        spread_kernel,
        in_specs=[SMEM] + [VMEM] * 5,
        out_specs=VMEM,
        out_shape=jax.ShapeDtypeStruct((8, 4, 48, 128), jnp.bfloat16),
        compiler_params=limit(16),
        cost_estimate=pl.CostEstimate(
            flops=2 * 256 * 1536 * 768, bytes_accessed=4 * 2**20, transcendentals=0
        ),
    )(place, rows, *pieces)


def collect_kernel(parts, out):
    total = jnp.sum(parts[...].astype(jnp.float32), axis=0).astype(jnp.bfloat16)
    rows = []
    for k in range(4):
        last = jnp.concatenate([total[k, 32:48, :64], total[k, 32:48, 64:]], axis=0)
        rows.append(jnp.concatenate([total[k, 0:32], last], axis=1))
    rows = jnp.concatenate(rows, axis=0)
    at = lax.broadcasted_iota(jnp.int32, (128, 128), 0)
    to = lax.broadcasted_iota(jnp.int32, (128, 128), 1)
    goes = ((at // 8) % 4) * 32 + (at // 64) * 16 + ((at // 2) % 4) * 4 + ((at // 32) % 2) * 2 + at % 2
    pick = jnp.where(goes == to, 1.0, 0.0).astype(jnp.bfloat16)
    out[...] = lax.dot_general(
        rows, pick, (((0,), (0,)), ((), ())), preferred_element_type=jnp.float32
    ).astype(jnp.bfloat16)


def collect(parts):
    return pl.pallas_call(
        collect_kernel,
        in_specs=[VMEM],
        out_specs=VMEM,
        compiler_params=limit(4),
        out_shape=jax.ShapeDtypeStruct((192, 128), jnp.bfloat16),
    )(parts)


OTHER = [(0, 1), (1, 0)]


def per_device(hidden, q_weight, kv_weight, o_weight, k_pool, v_pool, page_table, lengths):
    place = jnp.stack([lax.axis_index("zp"), lax.axis_index("c")])
    place = place.astype(jnp.int32)

    own = (q_weight.T, kv_weight.T)
    near = [lax.ppermute(part, "zp", OTHER) for part in own]
    pieces = (*own, *near, *(lax.ppermute(part, "c", OTHER) for part in (*own, *near)))
    o_own = o_weight.T
    o_near = lax.ppermute(o_own, "zp", OTHER)
    o_pieces = (o_own, o_near, lax.ppermute(o_own, "c", OTHER), lax.ppermute(o_near, "c", OTHER))

    rows = [
        lax.ppermute(
            part,
            G + ("zq", "zp", "c"),
            [
                ((g * 8 + z) * 2 + c, (z * 8 + g) * 2 + (c ^ flip))
                for g in range(8)
                for z in range(8)
                for c in range(2)
            ],
        )
        for flip, part in enumerate(split(place, hidden.T))
    ]
    rows = a2a(copies(place, *rows, near[0][:16, :128], near[1][:16, :128]), ("zq", "zp", "yh")).reshape(8, 4, 32, 384)

    parts = a2a(project(place, rows, pieces), G + ("zq", "yh")).reshape(8, 16, 2, 1024)
    first, second = (piece[:16, :128] for piece in o_pieces[2:])
    kv_rows, send = attend(page_table, lengths, parts, k_pool, v_pool, first, second)

    mine = a2a(send.reshape(128, 2, 1536), G + ("zq", "yh")).reshape(256, 1536)
    out = spread(place, mine, o_pieces)
    back = a2a(out.reshape(32, 48, 128), G + ("zp", "c")).reshape(8, 4, 48, 128)
    return (collect(back).T, kv_rows)


def solution(mesh):
    parts = Mesh(mesh.devices.reshape(2, 4, 4, 2, 4, 2), G + T)
    in_specs = (
        P(G, T),
        P(G, T),
        P(G, T),
        P(G, T),
        P(G + T, None, None),
        P(G + T, None, None),
        P(G + T, None),
        P(G + T),
    )
    out_specs = (P(G, T), P(G + T, None))
    return jax.shard_map(
        per_device, mesh=parts, in_specs=in_specs, out_specs=out_specs, check_vma=False
    )
```

```python
import jax
import jax.numpy as jnp
from jax import lax
from jax.experimental import pallas as pl
from jax.experimental.pallas import tpu as pltpu
from jax.sharding import Mesh, PartitionSpec as P

D = 12288
HD = 128

eps = 1e-05

G = ("yl", "x")
T = ("zq", "zp", "yh", "c")


def a2a(a, axes):
    return lax.all_to_all(a, axes, split_axis=0, concat_axis=0, tiled=True)


NT = (((1,), (1,)), ((), ()))
VMEM = pl.BlockSpec(memory_space=pltpu.VMEM)
SMEM = pl.BlockSpec(memory_space=pltpu.SMEM)


def in_hbm(a):
    return pltpu.with_memory_space_constraint(a, pltpu.HBM)


def limit(mib):
    return pltpu.CompilerParams(vmem_limit_bytes=mib * 2**20)


def split_kernel(place, hidden, own, other):
    row = lax.broadcasted_iota(jnp.int32, (64, 128), 0)
    col = lax.broadcasted_iota(jnp.int32, (64, 128), 1)
    for out, core in ((own, place[1]), (other, 1 - place[1])):
        goes = ((row // 8) % 4) * 32 + (row // 32) * 16 + ((row // 2) % 4) * 4 + core * 2 + row % 2
        pick = jnp.where(goes == col, 1.0, 0.0).astype(jnp.bfloat16)
        out[...] = lax.dot_general(
            pick, hidden[...], NT, preferred_element_type=jnp.float32
        ).astype(jnp.bfloat16)


def split(place, hidden):
    return pl.pallas_call(
        split_kernel,
        in_specs=[SMEM, VMEM],
        out_specs=[VMEM, VMEM],
        compiler_params=limit(4),
        out_shape=[jax.ShapeDtypeStruct((64, 192), jnp.bfloat16)] * 2,
    )(place, in_hbm(hidden))


def copies_kernel(place, own, other, first, second, out):
    del first, second
    flip = place[1] == 1
    first = jnp.where(flip, other[...], own[...])
    second = jnp.where(flip, own[...], other[...])
    both = jnp.concatenate([first, second], axis=1)
    for zq in range(4):
        for zp in range(2):
            for y in range(4):
                out[zq * 8 + zp * 4 + y] = both[zp * 32 : zp * 32 + 32]


def copies(place, own, other, first, second):
    return pl.pallas_call(
        copies_kernel,
        in_specs=[SMEM] + [VMEM] * 4,
        out_specs=VMEM,
        compiler_params=limit(4),
        out_shape=pltpu.HBM((32, 32, 384), jnp.bfloat16),
    )(place, own, other, first, second)


def project_kernel(place, rows, *refs):
    zp, core = place[0], place[1]
    out, weight, sem = refs[8:]
    fetches = []
    for y in range(4):
        part = slice(y * 384, y * 384 + 384)
        for k, (z, c) in enumerate(
            ((zp, core), (1 - zp, core), (zp, 1 - core), (1 - zp, 1 - core))
        ):
            at = z * 2 + c
            q_rows = pl.ds(pl.multiple_of(at * 192, 64), 192)
            kv_rows = pl.ds(pl.multiple_of(768 + at * 32, 32), 32)
            for j, to in enumerate((q_rows, kv_rows)):
                fetches.append(
                    pltpu.make_async_copy(
                        refs[2 * k + j].at[:, part],
                        weight.at[to, part],
                        sem.at[y * 8 + 2 * k + j],
                    )
                )
                fetches[-1].start()
    lane = lax.broadcasted_iota(jnp.int32, (128, 128), 1)
    extras = []
    for half in range(2):
        wide = 0
        for y in range(4):
            a = rows[half * 4 : half * 4 + 4, y].reshape(128, 384).astype(jnp.float32)
            a = a * a
            wide += a[:, :128] + a[:, 128:256] + a[:, 256:]
        sums = jnp.sum(wide, axis=1, keepdims=True)
        high = sums.astype(jnp.bfloat16).astype(jnp.float32)
        extras.append(jnp.where(lane == 0, high, jnp.where(lane == 1, sums - high, 0.0)))
    total = [0, 0]
    for y in range(4):
        for fetch in fetches[y * 8 : y * 8 + 8]:
            fetch.wait()
        for half in range(2):
            total[half] += lax.dot_general(
                rows[half * 4 : half * 4 + 4, y].reshape(128, 384),
                weight[:, y * 384 : y * 384 + 384],
                NT,
                preferred_element_type=jnp.float32,
            )
    for half in range(2):
        rounded = total[half].astype(jnp.bfloat16)
        extra = extras[half].astype(jnp.bfloat16)
        for r in range(64):
            at = slice(2 * r, 2 * r + 2)
            out[half * 64 + r, :, :896] = rounded[at]
            out[half * 64 + r, :, 896:] = extra[at]


def project(place, rows, pieces):
    return pl.pallas_call(
        project_kernel,
        in_specs=[SMEM, VMEM] + [pl.BlockSpec(memory_space=pl.ANY)] * 8,
        out_specs=VMEM,
        out_shape=pltpu.HBM((128, 2, 1024), jnp.bfloat16),
        scratch_shapes=[pltpu.VMEM((896, 1536), jnp.bfloat16), pltpu.SemaphoreType.DMA((32,))],
        compiler_params=limit(16),
        cost_estimate=pl.CostEstimate(
            flops=2 * 256 * 1536 * 896, bytes_accessed=4 * 2**20, transcendentals=0
        ),
    )(place, rows, *(in_hbm(piece) for piece in pieces))


def attend_kernel(table, lengths, parts, k_pool, v_pool, first, second, new_kv, send, query, mixed, v_held, sem, v_sem):
    del first, second
    fetch = pltpu.make_async_copy(v_pool, v_held, v_sem)
    fetch.start()
    row = lax.broadcasted_iota(jnp.int32, (24, 768), 0) % 2
    lane = lax.broadcasted_iota(jnp.int32, (1, 768), 1)
    masks = []
    for r in range(2):
        mask = jnp.zeros((1, 768), jnp.int32)
        for page in range(12):
            start = table[r, page] * 32
            end = start + jnp.clip(lengths[r] - page * 32, 0, 32)
            mask = jnp.where((lane >= start) & (lane < end), 1, mask)
        masks.append(mask)
    valid = jnp.where(row == 0, masks[0], masks[1]) == 1

    normed = []
    for k in range(16):
        total = jnp.sum(parts[:, k].astype(jnp.float32), axis=0)
        if k == 0:
            squares = jnp.sum(total[:, 896:], axis=1, keepdims=True)
            inv_rms = lax.rsqrt(squares / D + eps)
        normed.append((total[:, :896] * inv_rms).astype(jnp.bfloat16).astype(jnp.float32))
    for z in range(8):
        zq, zp = z // 2, z % 2
        for y in range(4):
            for k in range(3):
                at, h = zp * 384 + k * 128, y * 3 + k
                query[z, 2 * h : 2 * h + 2, :] = normed[zq * 4 + y][:, at : at + 128]
    fresh = []
    for z in range(8):
        at = 768 + (z % 2) * 64
        for y in range(0, 4, 2):
            pair = [normed[(z // 2) * 4 + y + k][:, at : at + 64] for k in range(2)]
            fresh.append(jnp.concatenate(pair, axis=1))
            to = z * 256 + y * 64
            new_kv[:, to : to + 128] = fresh[-1].astype(jnp.bfloat16)

    scale = 1.0 / jnp.sqrt(jnp.float32(HD))
    odd = lax.broadcasted_iota(jnp.int32, (24, 128), 0) % 2 == 1
    found = []
    for g in range(8):
        keys = k_pool[:, :, g * 128 : g * 128 + 128].reshape(768, 128)
        own_key = jnp.where(odd, fresh[g][1:2], fresh[g][0:1])
        q = query[g]
        scores = lax.dot_general(
            q.astype(jnp.bfloat16), keys, NT, preferred_element_type=jnp.float32
        )
        scores = jnp.where(valid, scores * scale, jnp.float32(-1e30))
        own = jnp.sum(q * own_key, axis=1, keepdims=True) * scale
        top = jnp.maximum(jnp.max(scores, axis=1, keepdims=True), own)
        scores = jnp.exp(scores - top)
        own = jnp.exp(own - top)
        total = jnp.sum(scores, axis=1, keepdims=True) + own
        inverse = 1.0 / total
        weights = (scores * inverse).astype(jnp.bfloat16)
        found.append((weights, (own * inverse).astype(jnp.bfloat16).astype(jnp.float32)))
    fetch.wait()
    copies = []
    for g, (weights, own) in enumerate(found):
        values = v_held[:, :, g * 128 : g * 128 + 128].reshape(768, 128)
        own_value = jnp.where(odd, fresh[8 + g][1:2], fresh[8 + g][0:1])
        out = lax.dot_general(
            weights, values, (((1,), (0,)), ((), ())), preferred_element_type=jnp.float32
        )
        out = (out + own * own_value).astype(jnp.bfloat16)
        for h in range(12):
            mixed[g, :, h * 128 : h * 128 + 128] = out[2 * h : 2 * h + 2]
        if g % 4 == 3:
            part = pl.ds(g - 3, 4)
            for k in range(16):
                copies.append(
                    pltpu.make_async_copy(
                        mixed.at[part], send.at[part, k], sem.at[g // 4 * 16 + k]
                    )
                )
                copies[-1].start()
    for copy in copies:
        copy.wait()


def attend(table, lengths, parts, k_pool, v_pool, first, second):
    return pl.pallas_call(
        attend_kernel,
        in_specs=[SMEM] * 2 + [VMEM] * 2 + [pl.BlockSpec(memory_space=pl.ANY)] + [VMEM] * 2,
        out_specs=[VMEM, pl.BlockSpec(memory_space=pl.ANY)],
        out_shape=[
            jax.ShapeDtypeStruct((2, 2048), jnp.bfloat16),
            pltpu.HBM((8, 16, 2, 1536), jnp.bfloat16),
        ],
        scratch_shapes=[
            pltpu.VMEM((8, 24, 128), jnp.float32),
            pltpu.VMEM((8, 2, 1536), jnp.bfloat16),
            pltpu.VMEM((24, 32, 1024), jnp.bfloat16),
            pltpu.SemaphoreType.DMA((32,)),
            pltpu.SemaphoreType.DMA,
        ],
        compiler_params=limit(16),
    )(table, lengths, parts, k_pool, in_hbm(v_pool), first, second)


def spread_kernel(place, rows, *refs):
    zp, core = place[0], place[1]
    out = refs[4]
    for k in range(4):
        weight = refs[k][...]
        z = zp if k % 2 == 0 else 1 - zp
        c = core if k < 2 else 1 - core
        part = lax.dot_general(rows[...], weight, NT, preferred_element_type=jnp.float32)
        part = part.astype(jnp.bfloat16)
        for g in range(8):
            at = g * 32
            out[g, z * 2 + c, 0:32, :] = part[at : at + 32, :128]
            out[g, z * 2 + c, 32:48, :] = jnp.concatenate(
                [part[at : at + 16, 128:], part[at + 16 : at + 32, 128:]], axis=1
            )


def spread(place, rows, pieces):
    return pl.pallas_call(
        spread_kernel,
        in_specs=[SMEM] + [VMEM] * 5,
        out_specs=VMEM,
        out_shape=jax.ShapeDtypeStruct((8, 4, 48, 128), jnp.bfloat16),
        compiler_params=limit(16),
        cost_estimate=pl.CostEstimate(
            flops=2 * 256 * 1536 * 768, bytes_accessed=4 * 2**20, transcendentals=0
        ),
    )(place, rows, *pieces)


def collect_kernel(parts, out):
    total = jnp.sum(parts[...].astype(jnp.float32), axis=0).astype(jnp.bfloat16)
    rows = []
    for k in range(4):
        last = jnp.concatenate([total[k, 32:48, :64], total[k, 32:48, 64:]], axis=0)
        rows.append(jnp.concatenate([total[k, 0:32], last], axis=1))
    rows = jnp.concatenate(rows, axis=0)
    at = lax.broadcasted_iota(jnp.int32, (128, 128), 0)
    to = lax.broadcasted_iota(jnp.int32, (128, 128), 1)
    goes = ((at // 8) % 4) * 32 + (at // 64) * 16 + ((at // 2) % 4) * 4 + ((at // 32) % 2) * 2 + at % 2
    pick = jnp.where(goes == to, 1.0, 0.0).astype(jnp.bfloat16)
    out[...] = lax.dot_general(
        rows, pick, (((0,), (0,)), ((), ())), preferred_element_type=jnp.float32
    ).astype(jnp.bfloat16)


def collect(parts):
    return pl.pallas_call(
        collect_kernel,
        in_specs=[VMEM],
        out_specs=VMEM,
        compiler_params=limit(4),
        out_shape=jax.ShapeDtypeStruct((192, 128), jnp.bfloat16),
    )(parts)


OTHER = [(0, 1), (1, 0)]


def per_device(hidden, q_weight, kv_weight, o_weight, k_pool, v_pool, page_table, lengths):
    place = jnp.stack([lax.axis_index("zp"), lax.axis_index("c")])
    place = place.astype(jnp.int32)

    own = (q_weight.T, kv_weight.T)
    near = [lax.ppermute(part, "zp", OTHER) for part in own]
    pieces = (*own, *near, *(lax.ppermute(part, "c", OTHER) for part in (*own, *near)))
    o_own = o_weight.T
    o_near = lax.ppermute(o_own, "zp", OTHER)
    o_pieces = (o_own, o_near, lax.ppermute(o_own, "c", OTHER), lax.ppermute(o_near, "c", OTHER))

    rows = [
        lax.ppermute(
            part,
            G + ("zq", "zp", "c"),
            [
                ((g * 8 + z) * 2 + c, (z * 8 + g) * 2 + (c ^ flip))
                for g in range(8)
                for z in range(8)
                for c in range(2)
            ],
        )
        for flip, part in enumerate(split(place, hidden.T))
    ]
    rows = a2a(copies(place, *rows, near[0][:16, :128], near[1][:16, :128]), ("zq", "zp", "yh")).reshape(8, 4, 32, 384)

    parts = a2a(project(place, rows, pieces), G + ("zq", "yh")).reshape(8, 16, 2, 1024)
    first, second = (piece[:16, :128] for piece in o_pieces[2:])
    kv_rows, send = attend(page_table, lengths, parts, k_pool, v_pool, first, second)

    mine = a2a(send.reshape(128, 2, 1536), G + ("zq", "yh")).reshape(256, 1536)
    out = spread(place, mine, o_pieces)
    back = a2a(out.reshape(32, 48, 128), G + ("zp", "c")).reshape(8, 4, 48, 128)
    return (collect(back).T, kv_rows)


def solution(mesh):
    parts = Mesh(mesh.devices.reshape(2, 4, 4, 2, 4, 2), G + T)
    in_specs = (
        P(G, T),
        P(G, T),
        P(G, T),
        P(G, T),
        P(G + T, None, None),
        P(G + T, None, None),
        P(G + T, None),
        P(G + T),
    )
    out_specs = (P(G, T), P(G + T, None))
    return jax.shard_map(
        per_device, mesh=parts, in_specs=in_specs, out_specs=out_specs, check_vma=False
    )
```
